32 devices in a mesh: gx: 8 (over z, x), gy: 4 (over y, core).
Axes of the slice: x: 2, y: 2, z: 4, core: 2. Of those that a mesh axis runs over, the one named last changes fastest.
Arguments:
- resident_rows: int32 [4, 8, 32768], P('gy', 'gx'), may hold values from 0 to 1023
- resident_columns: int32 [4, 8, 32768], P('gy', 'gx'), may hold values from 0 to 511
- resident_strength: float32 [3, 4, 8, 32768], P(None, 'gy', 'gx'), may hold values from -6 to 6
- crossing_rows: int32 [4, 8, 2048], P('gy', 'gx'), may hold values from 0 to 1023
- crossing_columns: int32 [4, 8, 2048], P('gy', 'gx'), may hold values from 0 to 511
- crossing_strength: float32 [3, 4, 8, 2048], P(None, 'gy', 'gx'), may hold values from -6 to 6
- crossing_count: int32 [4, 8], P('gy', 'gx'), may hold values from 512 to 2048, as said below
Outputs:
- vorticity_spectrum: float32 [2, 3, 1, 4096, 4096], P(None, None, None, 'gy', 'gx')
The draws below stay inside these ranges and needn't reach their ends.
Inputs may be any that keep to these rules, and one draw needn't show every extreme that they name: `crossing_count`: in every draw at least one device has exactly 2048 live send slots.
All inputs are finite; a program needn't handle non-finite values.
Results may differ from the reference program's by a relative error of at most 0.0003.
Values sent between devices are 32-bit elements; how exact they have to be, the bound alone decides.
No kernel may reach another device: no remote copies, remote signals or barrier semaphores. Data moves between devices by JAX's collectives and lax.ppermute only.
A program may use at most 192 MiB of HBM per device.

```python
import jax
import jax.numpy as jnp
import numpy as np
from jax import lax

NX = 4096
NY = 4096
LEV = 1
PART_DEV = 32768
CAP = 2048
SLABS_X = 8
SLABS_Y = 4
CX_DEV = 512
CY_DEV = 1024
N_GX = 8
N_GY = 4


def draw_crossing_count(key, part):
    spread_key = jax.random.fold_in(key, 11)
    pick_key = jax.random.fold_in(key, 23)
    counts = jax.random.randint(spread_key, (SLABS_Y, SLABS_X), CAP // 4, CAP + 1, dtype=jnp.int32)
    chosen = jax.random.randint(pick_key, (), 0, SLABS_Y * SLABS_X, dtype=jnp.int32)
    flat_index = lax.broadcasted_iota(jnp.int32, (SLABS_Y, SLABS_X), 0) * SLABS_X + lax.broadcasted_iota(jnp.int32, (SLABS_Y, SLABS_X), 1)
    return jnp.where(flat_index == chosen, jnp.int32(CAP), counts)


def place_ends(values, key, low, largest):
    index_at = [jax.random.randint(jax.random.fold_in(key, axis), (), 0, length) for axis, length in enumerate(values.shape)]
    main_axis = values.shape.index(max(values.shape))
    neighbour = index_at[:main_axis] + [(index_at[main_axis] + 1) % values.shape[main_axis]] + index_at[main_axis + 1:]
    return values.at[tuple(index_at)].set(low).at[tuple(neighbour)].set(largest)


def levels(key, dims, cuts, low, top_value):
    gain = 1.0
    for axis_at, blocks in cuts:
        heights = jax.random.uniform(jax.random.fold_in(jax.random.fold_in(key, 6), axis_at), (blocks,), jnp.float32, low / len(cuts), top_value / len(cuts))
        gain = gain * jnp.repeat(jnp.exp(heights), dims[axis_at] // blocks).reshape((-1,) + (1,) * (len(dims) - 1 - axis_at))
    return gain


def bell_draw(stream_key, shape, deviation, limit, split=(), kind=jnp.bfloat16):
    entries = jax.random.normal(stream_key, shape, jnp.float32) * deviation
    if len(split) > 0:
        entries = levels(stream_key, shape, split, -0.22, 0.18) * entries
    return jnp.clip(entries, min=-limit, max=limit).astype(kind)


def setup_inputs(seed: int = 0) -> dict:
    key_of = jax.random.split(jax.random.key(seed), 8)
    return {
        "resident_rows": place_ends(jax.random.randint(key_of[0], (SLABS_Y, SLABS_X, PART_DEV), 0, LEV * CY_DEV), jax.random.fold_in(key_of[0], 1), 0, (LEV * CY_DEV) - 1).astype(jnp.int32),
        "resident_columns": place_ends(jax.random.randint(key_of[1], (SLABS_Y, SLABS_X, PART_DEV), 0, CX_DEV), jax.random.fold_in(key_of[1], 1), 0, CX_DEV - 1).astype(jnp.int32),
        "resident_strength": bell_draw(key_of[2], (3, SLABS_Y, SLABS_X, PART_DEV), 1.0, 6.0, ((1, 4), (2, 8)), jnp.float32),
        "crossing_rows": place_ends(jax.random.randint(key_of[3], (SLABS_Y, SLABS_X, CAP), 0, LEV * CY_DEV), jax.random.fold_in(key_of[3], 1), 0, (LEV * CY_DEV) - 1).astype(jnp.int32),
        "crossing_columns": place_ends(jax.random.randint(key_of[4], (SLABS_Y, SLABS_X, CAP), 0, CX_DEV), jax.random.fold_in(key_of[4], 1), 0, CX_DEV - 1).astype(jnp.int32),
        "crossing_strength": bell_draw(key_of[5], (3, SLABS_Y, SLABS_X, CAP), 1.0, 6.0, ((1, 4), (2, 8)), jnp.float32),
        "crossing_count": draw_crossing_count(jax.random.fold_in(key_of[7], 71), 0),
    }


def reverse_bits(slab_count):
    bit_count = slab_count.bit_length() - 1
    values = np.arange(slab_count)
    result = np.zeros(slab_count, dtype=np.int64)
    for level in range(bit_count):
        result = result | (((values >> level) & 1) << (bit_count - 1 - level))
    return result


def spectrum_order(length, slab_count):
    width = length // slab_count
    reversed_slabs = reverse_bits(slab_count)
    return (reversed_slabs[:, None] + slab_count * np.arange(width)[None, :]).reshape(-1)


def reference(resident_rows, resident_columns, resident_strength, crossing_rows, crossing_columns, crossing_strength, crossing_count):
    cells_x = NX // N_GX
    cells_y = NY // N_GY
    slab_y = jnp.arange(N_GY, dtype=jnp.int32).reshape(N_GY, 1, 1)
    slab_x = jnp.arange(N_GX, dtype=jnp.int32).reshape(1, N_GX, 1)

    def global_index(local_rows, local_columns, target_x):
        level_of = local_rows // cells_y
        row_in = local_rows % cells_y
        return ((level_of * NY + slab_y * cells_y + row_in) * NX + target_x * cells_x + local_columns).astype(jnp.int32)

    resident_global = global_index(resident_rows, resident_columns, slab_x)
    crossing_global = global_index(crossing_rows, crossing_columns, (slab_x + 1) % N_GX)
    slot_index = jnp.arange(CAP, dtype=jnp.int32).reshape(1, 1, CAP)
    live_slot = (slot_index < crossing_count[:, :, None]).astype(jnp.float32)
    crossing_weights = crossing_strength * live_slot[None]
    cell_ids = jnp.concatenate([resident_global.reshape(-1), crossing_global.reshape(-1)])
    weights = jnp.concatenate([resident_strength.reshape(3, -1), crossing_weights.reshape(3, -1)], axis=1)
    vorticity = jax.ops.segment_sum(weights.T, cell_ids, num_segments=LEV * NY * NX).T.reshape(3, LEV, NY, NX)
    order_y = jnp.asarray(spectrum_order(NY, N_GY), dtype=jnp.int32)
    order_x = jnp.asarray(spectrum_order(NX, N_GX), dtype=jnp.int32)

    def transform_one(component):
        spectrum = jnp.fft.fft2(component, norm="ortho")
        spectrum = jnp.take(spectrum, order_y, axis=1)
        spectrum = jnp.take(spectrum, order_x, axis=2)
        return jnp.stack([jnp.real(spectrum), jnp.imag(spectrum)]).astype(jnp.float32)

    result = lax.map(transform_one, vorticity)
    return jnp.moveaxis(result, 1, 0)
```

```python
import math

import jax
import jax.numpy as jnp
from jax import lax
from jax.experimental import pallas as pl
from jax.experimental.pallas import tpu as pltpu
from jax.sharding import PartitionSpec as P

NX = 4096
NY = 4096
LEV = 1


TWO_PI = 2.0 * math.pi

BIN_ROWS = 256
BIN_COLS = 32
CHUNK = 256
LANES = 128


def from_behind(value, axis, steps):
    count = lax.axis_size(axis)
    pairs = [(source, (source + steps) % count) for source in range(count)]
    return lax.ppermute(value, axis, pairs)


def flip(value, axis, mask):
    count = lax.axis_size(axis)
    return lax.ppermute(value, axis, [(source, source ^ mask) for source in range(count)])


def bit_reverse(slab_index, bit_count):
    result = jnp.zeros_like(slab_index)
    for level in range(bit_count):
        result = result | (slab_index >> level & 1) << bit_count - 1 - level
    return result


def partner_2(block, axis, stride):
    count = lax.axis_size(axis)
    route = []
    for low in range(count):
        high = low | 1 << stride
        if high != low and high < count:
            route += [(low, high), (high, low)]
    return lax.ppermute(block, axis, route)


def section_mix(parts, partner, slab_index, bit_number):
    half_span = 1 << bit_number
    upper_half = slab_index >> bit_number & 1 == 1
    phase_angle = (slab_index & half_span - 1).astype(jnp.float32) * (-math.pi / half_span)
    cosine = jnp.cos(phase_angle)
    sine_value = jnp.sin(phase_angle)
    summed = parts + partner
    difference = partner - parts
    if parts.shape[0] == 1:
        summed = jnp.concatenate([summed, jnp.zeros_like(summed)])
        turned = jnp.concatenate([difference * cosine, difference * sine_value])
    else:
        turned = jnp.stack(
            [
                difference[0] * cosine - difference[1] * sine_value,
                difference[0] * sine_value + difference[1] * cosine,
            ]
        )
    return jnp.where(upper_half, turned, summed)


def local_table(k_first, slab_count, length):
    total = slab_count * length
    row_index = lax.broadcasted_iota(jnp.int32, (length, length), 0)
    col_index = lax.broadcasted_iota(jnp.int32, (length, length), 1)
    phase = col_index * (k_first + slab_count * row_index) % total
    phase_angle = phase.astype(jnp.float32) * (TWO_PI / total)
    return (jnp.cos(phase_angle), -jnp.sin(phase_angle))


def along(parts, table_real, table_imag, spec):
    def product(data, table):
        return jnp.einsum(
            spec,
            data,
            table,
            precision=lax.Precision.HIGHEST,
            preferred_element_type=jnp.float32,
        )

    return jnp.stack(
        [
            product(parts[0], table_real) - product(parts[1], table_imag),
            product(parts[0], table_imag) + product(parts[1], table_real),
        ]
    )


def dense_shards(
    resident_rows,
    resident_columns,
    resident_strength,
    crossing_rows,
    crossing_columns,
    crossing_strength,
    crossing_count,
):
    cells_x = NX // lax.axis_size("gx")
    cells_y = NY // lax.axis_size("gy")
    slot_count = crossing_rows.shape[-1]
    slot_index = lax.broadcasted_iota(jnp.int32, (1, slot_count), 1)
    live_slot = (slot_index < crossing_count).astype(jnp.float32)
    outgoing = jnp.concatenate(
        [
            crossing_rows.reshape(1, slot_count).astype(jnp.float32),
            crossing_columns.reshape(1, slot_count).astype(jnp.float32),
            crossing_strength.reshape(3, slot_count) * live_slot,
        ],
        axis=0,
    )
    arrived = from_behind(outgoing, "gx", 1)
    resident_ids = resident_rows.reshape(-1) * cells_x + resident_columns.reshape(-1)
    arrived_ids = arrived[0].astype(jnp.int32) * cells_x + arrived[1].astype(jnp.int32)
    cell_ids = jnp.concatenate([resident_ids, arrived_ids])
    weights = jnp.concatenate([resident_strength.reshape(3, -1), arrived[2:]], axis=1)
    cell_total = LEV * cells_y * cells_x
    deposited = jnp.stack(
        [
            jax.ops.segment_sum(weights[component], cell_ids, num_segments=cell_total)
            for component in range(3)
        ]
    )
    vorticity = deposited.reshape(1, 3, LEV, cells_y, cells_x) * (1.0 / math.sqrt(NX * NY))
    parts = vorticity
    for axis, cells, spec in (
        ("gx", cells_x, "clyx,kx->clyk"),
        ("gy", cells_y, "clyx,ky->clkx"),
    ):
        bits = lax.axis_size(axis).bit_length() - 1
        slab_index = lax.axis_index(axis)
        for bit_number in range(bits - 1, -1, -1):
            partner = partner_2(parts, axis, bit_number)
            parts = section_mix(parts, partner, slab_index, bit_number)
        table_real, table_imag = local_table(bit_reverse(slab_index, bits), 1 << bits, cells)
        parts = along(parts, table_real, table_imag, spec)
    return parts


def bin_key(rows, columns, cells_x):
    column = (columns & 1) * (cells_x // 2) + (columns >> 1)
    bin_index = (column // BIN_COLS) * 4 + (rows & 3)
    return bin_index * (BIN_ROWS * BIN_COLS) + (rows >> 2) * BIN_COLS + column % BIN_COLS


def deposit(sources, signs, cells_x, cells_y):
    count = len(sources)
    row_bins = cells_y // BIN_ROWS
    col_bins = cells_x // BIN_COLS
    bins = row_bins * col_bins
    width = sources[0].shape[-1]
    first_start = width - LANES
    shift = BIN_COLS.bit_length() - 1
    starts = jnp.stack(
        [source[0, first_start : first_start + bins + 1] for source in sources]
    ).astype(jnp.int32)

    def kernel(starts_ref, signs_ref, *refs):
        source_refs, out_ref = refs[:count], refs[count]
        group = pl.program_id(0)
        spans = []
        steps = jnp.int32(0)
        for row_bin in range(row_bins):
            bin_index = group * row_bins + row_bin
            for s in range(count):
                begin = starts_ref[s, bin_index]
                end = starts_ref[s, bin_index + 1]
                aligned = (begin // LANES) * LANES
                spans.append((aligned, begin, end))
                steps = jnp.maximum(steps, (end - aligned + CHUNK - 1) // CHUNK)
        lane = lax.broadcasted_iota(jnp.int32, (1, CHUNK), 1)

        def ramp(length):
            return (
                lax.broadcasted_iota(jnp.int32, (length, CHUNK), 0)
                .astype(jnp.float32)
                .astype(jnp.bfloat16)
            )

        row_ramp, col_ramp = ramp(BIN_ROWS), ramp(BIN_COLS)
        one, zero = jnp.bfloat16(1), jnp.bfloat16(0)

        def body(step, carry):
            totals = []
            for row_bin in range(row_bins):
                base = (group * row_bins + row_bin) * (BIN_ROWS * BIN_COLS)
                hits, weights = [], []
                for s in range(count):
                    aligned, begin, end = spans[row_bin * count + s]
                    here = aligned + step * CHUNK
                    offset = pl.multiple_of(jnp.minimum(here, width - CHUNK), LANES)
                    block = source_refs[s][:, pl.ds(offset, CHUNK)]
                    place = lane + offset
                    valid = (place >= jnp.maximum(begin, here)) & (place < end)
                    local = block[0:1].astype(jnp.int32) - base
                    row = jnp.where(valid, lax.shift_right_arithmetic(local, shift), -1)
                    col = local & (BIN_COLS - 1)
                    row = row.astype(jnp.float32).astype(jnp.bfloat16)
                    col = col.astype(jnp.float32).astype(jnp.bfloat16)
                    hits.append(jnp.where(row_ramp == row, one, zero))
                    mask = col_ramp == col
                    value = block * signs_ref[s]
                    high = value.astype(jnp.bfloat16)
                    low = (value - high.astype(jnp.float32)).astype(jnp.bfloat16)
                    weights.append(
                        jnp.concatenate(
                            [
                                jnp.where(
                                    mask,
                                    jnp.broadcast_to(piece[k : k + 1], (BIN_COLS, CHUNK)),
                                    zero,
                                )
                                for piece in (high, low)
                                for k in (1, 2, 3)
                            ],
                            axis=0,
                        )
                    )
                total = lax.dot_general(
                    jnp.concatenate(weights, axis=1),
                    jnp.concatenate(hits, axis=1),
                    (((1,), (1,)), ((), ())),
                    preferred_element_type=jnp.float32,
                )
                totals.append(total[: 3 * BIN_COLS] + total[3 * BIN_COLS :])
            for row_bin in range(row_bins):
                where = slice(row_bin * BIN_ROWS, (row_bin + 1) * BIN_ROWS)
                out_ref[:, :, where] += totals[row_bin].reshape(3, BIN_COLS, BIN_ROWS)
            return carry

        out_ref[...] = jnp.zeros_like(out_ref)
        lax.fori_loop(0, steps, body, 0)

    flops = count * width * BIN_ROWS * BIN_COLS * 12
    return pl.pallas_call(
        kernel,
        grid_spec=pltpu.PrefetchScalarGridSpec(
            num_scalar_prefetch=1,
            grid=(col_bins,),
            in_specs=[pl.BlockSpec(memory_space=pltpu.SMEM)]
            + [pl.BlockSpec(memory_space=pltpu.VMEM)] * count,
            out_specs=pl.BlockSpec((3, BIN_COLS, cells_y), lambda g, starts: (0, g, 0)),
        ),
        out_shape=jax.ShapeDtypeStruct((3, cells_x, cells_y), jnp.float32),
        compiler_params=pltpu.CompilerParams(vmem_limit_bytes=40 << 20),
        cost_estimate=pl.CostEstimate(
            flops=flops * 2, bytes_accessed=12 * cells_x * cells_y, transcendentals=0
        ),
        name="deposit",
    )(starts, signs, *sources)


def turns(numerator, total):
    angle = (numerator % total).astype(jnp.float32) * (TWO_PI / total)
    return jnp.cos(angle), -jnp.sin(angle)


def stage_table(k_first, slab_count, radix, length):
    total = slab_count * radix * length
    shape = (radix, length, length)
    residue = lax.broadcasted_iota(jnp.int32, shape, 0)
    k = k_first + slab_count * lax.broadcasted_iota(jnp.int32, shape, 1)
    n = radix * lax.broadcasted_iota(jnp.int32, shape, 2) + residue
    real, imag = turns(k * n, total)
    return jnp.concatenate(
        [jnp.concatenate([real, -imag], axis=2), jnp.concatenate([imag, real], axis=2)], axis=1
    )


def split(value):
    high = value.astype(jnp.bfloat16)
    return high, (value - high.astype(jnp.float32)).astype(jnp.bfloat16)


def fill_tables(table_ref, held_ref, radix):
    for residue in range(radix):
        high, low = split(table_ref[residue])
        held_ref[residue] = jnp.concatenate([high, high, low], axis=1)


def columns_transform(meshes, scalars, table, component, block):
    count = len(meshes)
    cells_x, cells_y = meshes[0].shape[1:]
    half = cells_x // 2

    def kernel(scalars_ref, table_ref, *refs):
        mesh_refs, out_ref, held_ref = refs[:count], refs[count], refs[count + 1]

        @pl.when(pl.program_id(0) == 0)
        def _():
            fill_tables(table_ref, held_ref, 2)

        pieces = []
        for residue in range(2):
            rows = slice(residue * half, (residue + 1) * half)
            data = [mesh_ref[0, rows, :] for mesh_ref in mesh_refs]
            real = sum(scalars_ref[0, i] * data[i] for i in range(count))
            imag = sum(scalars_ref[1, i] * data[i] for i in range(count))
            high, low = split(jnp.concatenate([real, imag], axis=0))
            pieces.append(
                jnp.dot(
                    held_ref[residue],
                    jnp.concatenate([high, low, high], axis=0),
                    preferred_element_type=jnp.float32,
                )
            )
        for part in range(2):
            rows = slice(part * half, (part + 1) * half)
            out_ref[part, 0, :half] = pieces[0][rows] + pieces[1][rows]
            out_ref[part, 0, half:] = pieces[0][rows] - pieces[1][rows]

    return pl.pallas_call(
        kernel,
        grid=(cells_y // block,),
        in_specs=[
            pl.BlockSpec(memory_space=pltpu.SMEM),
            pl.BlockSpec(memory_space=pltpu.VMEM),
        ]
        + [pl.BlockSpec((1, cells_x, block), lambda g: (component, 0, g))] * count,
        out_specs=pl.BlockSpec((2, 1, cells_x, block), lambda g: (0, 0, 0, g)),
        out_shape=jax.ShapeDtypeStruct((2, 1, cells_x, cells_y), jnp.float32),
        scratch_shapes=[pltpu.VMEM((2, cells_x, 3 * cells_x), jnp.bfloat16)],
        compiler_params=pltpu.CompilerParams(vmem_limit_bytes=40 << 20),
        cost_estimate=pl.CostEstimate(
            flops=12 * cells_x * cells_x * cells_y,
            bytes_accessed=(count + 2) * 4 * cells_x * cells_y,
            transcendentals=0,
        ),
        name="columns_transform",
    )(scalars, table, *meshes)


def rows_transform(owns, partners, scalars, table, block):
    count = len(owns)
    cells_x, cells_y = owns[0].shape[2:]
    quarter = cells_y // 4

    def kernel(scalars_ref, table_ref, *refs):
        own_refs, partner_refs = refs[:count], refs[count : 2 * count]
        out_ref, held_ref = refs[2 * count :]

        @pl.when(pl.program_id(0) == 0)
        def _():
            fill_tables(table_ref, held_ref, 4)

        own_real, own_imag = scalars_ref[0], scalars_ref[1]
        other_real, other_imag = scalars_ref[2], scalars_ref[3]
        for c in range(count):
            pieces = []
            for residue in range(4):
                where = slice(residue * quarter, (residue + 1) * quarter)
                a, b = own_refs[c][0, 0, :, where], own_refs[c][1, 0, :, where]
                d, e = partner_refs[c][0, 0, :, where], partner_refs[c][1, 0, :, where]
                real = own_real * a - own_imag * b + other_real * d - other_imag * e
                imag = own_real * b + own_imag * a + other_real * e + other_imag * d
                high, low = split(jnp.concatenate([real, imag], axis=1))
                piece = lax.dot_general(
                    held_ref[residue],
                    jnp.concatenate([high, low, high], axis=1),
                    (((1,), (1,)), ((), ())),
                    preferred_element_type=jnp.float32,
                )
                pieces.append((piece[:quarter], piece[quarter:]))
            (ar, ai), (br, bi), (cr, ci), (dr, di) = pieces
            even_r, even_i, odd_r, odd_i = ar + cr, ai + ci, br + dr, bi + di
            diff_r, diff_i, turn_r, turn_i = ar - cr, ai - ci, br - dr, bi - di
            out_ref[0, c, 0, 0 * quarter : 1 * quarter] = even_r + odd_r
            out_ref[1, c, 0, 0 * quarter : 1 * quarter] = even_i + odd_i
            out_ref[0, c, 0, 1 * quarter : 2 * quarter] = diff_r + turn_i
            out_ref[1, c, 0, 1 * quarter : 2 * quarter] = diff_i - turn_r
            out_ref[0, c, 0, 2 * quarter : 3 * quarter] = even_r - odd_r
            out_ref[1, c, 0, 2 * quarter : 3 * quarter] = even_i - odd_i
            out_ref[0, c, 0, 3 * quarter : 4 * quarter] = diff_r - turn_i
            out_ref[1, c, 0, 3 * quarter : 4 * quarter] = diff_i + turn_r

    spec = pl.BlockSpec((2, 1, block, cells_y), lambda g: (0, 0, g, 0))
    return pl.pallas_call(
        kernel,
        grid=(cells_x // block,),
        in_specs=[
            pl.BlockSpec(memory_space=pltpu.SMEM),
            pl.BlockSpec(memory_space=pltpu.VMEM),
        ]
        + [spec] * (2 * count),
        out_specs=pl.BlockSpec((2, count, 1, cells_y, block), lambda g: (0, 0, 0, 0, g)),
        out_shape=jax.ShapeDtypeStruct((2, count, 1, cells_y, cells_x), jnp.float32),
        scratch_shapes=[pltpu.VMEM((4, 2 * quarter, 6 * quarter), jnp.bfloat16)],
        compiler_params=pltpu.CompilerParams(vmem_limit_bytes=52 << 20),
        cost_estimate=pl.CostEstimate(
            flops=count * 6 * cells_y * cells_y * cells_x,
            bytes_accessed=count * 24 * cells_x * cells_y,
            transcendentals=0,
        ),
        name="rows_transform",
    )(scalars, table, *owns, *partners)


def particle_shards(
    resident_rows,
    resident_columns,
    resident_strength,
    crossing_rows,
    crossing_columns,
    crossing_strength,
    crossing_count,
):
    cells_x = NX // lax.axis_size("gx")
    cells_y = NY // lax.axis_size("gy")
    bins = (cells_y // BIN_ROWS) * (cells_x // BIN_COLS)
    gx, gy = lax.axis_index("gx"), lax.axis_index("gy")
    x, z = gx & 1, gx >> 1
    core, y = gy & 1, gy >> 1
    kx_first = bit_reverse(gx, 3)
    ky_first = bit_reverse(gy, 2)

    slot_count = crossing_rows.shape[-1]
    slot_index = lax.broadcasted_iota(jnp.int32, (1, slot_count), 1)
    live_slot = (slot_index < crossing_count).astype(jnp.float32)
    crossing_key = bin_key(crossing_rows.reshape(1, -1), crossing_columns.reshape(1, -1), cells_x)
    outgoing = jnp.concatenate(
        [crossing_key.astype(jnp.float32), crossing_strength.reshape(3, slot_count) * live_slot]
    )
    arrived = from_behind(outgoing, "gx", 1)
    resident_key = bin_key(resident_rows.reshape(-1), resident_columns.reshape(-1), cells_x)
    key = jnp.concatenate([resident_key, arrived[0].astype(jnp.int32)])
    strength = [
        jnp.concatenate([resident_strength[i].reshape(-1), arrived[1 + i]]) for i in range(3)
    ]
    key, *strength = lax.sort((key, *strength), num_keys=1, is_stable=False)
    bounds = lax.broadcasted_iota(jnp.int32, (LANES, 1), 0) * (BIN_ROWS * BIN_COLS)
    starts = jnp.sum((key[None, :] < bounds).astype(jnp.int32), axis=1)
    particles = jnp.concatenate(
        [
            jnp.stack([key.astype(jnp.float32), *strength]),
            jnp.concatenate([starts.astype(jnp.float32)[None], jnp.zeros((3, LANES), jnp.float32)]),
        ],
        axis=1,
    )

    near = {0: particles}
    far = {0: flip(particles, "gy", 2)}
    near[4] = flip(near[0], "gx", 4)
    far[4] = flip(near[4], "gy", 2)
    near[1] = flip(near[0], "gx", 1)
    far[1] = flip(far[0], "gx", 1)
    near[5] = flip(near[4], "gx", 1)
    far[5] = flip(near[5], "gy", 2)
    near[2] = flip(near[0], "gx", 2)
    far[2] = flip(far[0], "gx", 2)
    near[6] = flip(near[0], "gx", 6)
    far[6] = flip(near[6], "gy", 2)
    near[3] = flip(near[2], "gx", 1)
    far[3] = flip(near[3], "gy", 2)
    near[7] = flip(near[6], "gx", 1)
    far[7] = flip(far[6], "gx", 1)

    meshes, scalars = [], []
    kx_low = kx_first & 3
    for k in (0, 1, 2, 3):
        slab_x = x ^ (k & 1)
        slab_z = z ^ (k >> 1)
        signs = []
        for top in (0, 2):
            for slab_y in (y, 1 - y):
                flips = kx_low * ((slab_z ^ top) >> 1) + y * slab_y
                signs.append((1 - 2 * (flips & 1)).astype(jnp.float32))
        meshes.append(
            deposit(
                [near[k], far[k], near[k ^ 4], far[k ^ 4]], jnp.stack(signs), cells_x, cells_y
            )
        )
        real, imag = turns(kx_first * slab_x + 2 * kx_low * (slab_z & 1), 8)
        scalars.append(jnp.stack([real, imag]) * (1.0 / math.sqrt(NX * NY)))
    scalars = jnp.stack(scalars, axis=1)

    table = stage_table(kx_first, 8, 2, cells_x // 2)
    owns = [columns_transform(meshes, scalars, table, i, 256) for i in range(3)]
    partners = [flip(own, "gy", 1) for own in owns]

    turn_real, turn_imag = turns(ky_first, 4)
    low = core == 0
    scalars = jnp.stack(
        [
            jnp.where(low, 1.0, turn_real),
            jnp.where(low, 0.0, turn_imag),
            jnp.where(low, turn_real, 1.0),
            jnp.where(low, turn_imag, 0.0),
        ]
    )
    table = stage_table(ky_first, 4, 4, cells_y // 4)
    return rows_transform(owns, partners, scalars, table, 128)


def solution(mesh):
    few = mesh.shape["gx"] == 8 and mesh.shape["gy"] == 4
    return jax.shard_map(
        particle_shards if few else dense_shards,
        mesh=mesh,
        in_specs=(
            P("gy", "gx", None),
            P("gy", "gx", None),
            P(None, "gy", "gx", None),
            P("gy", "gx", None),
            P("gy", "gx", None),
            P(None, "gy", "gx", None),
            P("gy", "gx"),
        ),
        out_specs=P(None, None, None, "gy", "gx"),
        check_vma=False,
    )
```

```python
import math

import jax
import jax.numpy as jnp
from jax import lax
from jax.experimental import pallas as pl
from jax.experimental.pallas import tpu as pltpu
from jax.sharding import PartitionSpec as P

NX = 4096
NY = 4096
LEV = 1


TWO_PI = 2.0 * math.pi

BIN_ROWS = 256
BIN_COLS = 32
CHUNK = 640
LANES = 128


def from_behind(value, axis, steps):
    count = lax.axis_size(axis)
    pairs = [(source, (source + steps) % count) for source in range(count)]
    return lax.ppermute(value, axis, pairs)


def flip(value, axis, mask):
    count = lax.axis_size(axis)
    return lax.ppermute(value, axis, [(source, source ^ mask) for source in range(count)])


def bit_reverse(slab_index, bit_count):
    result = jnp.zeros_like(slab_index)
    for level in range(bit_count):
        result = result | (slab_index >> level & 1) << bit_count - 1 - level
    return result


def partner_2(block, axis, stride):
    count = lax.axis_size(axis)
    route = []
    for low in range(count):
        high = low | 1 << stride
        if high != low and high < count:
            route += [(low, high), (high, low)]
    return lax.ppermute(block, axis, route)


def section_mix(parts, partner, slab_index, bit_number):
    half_span = 1 << bit_number
    upper_half = slab_index >> bit_number & 1 == 1
    phase_angle = (slab_index & half_span - 1).astype(jnp.float32) * (-math.pi / half_span)
    cosine = jnp.cos(phase_angle)
    sine_value = jnp.sin(phase_angle)
    summed = parts + partner
    difference = partner - parts
    if parts.shape[0] == 1:
        summed = jnp.concatenate([summed, jnp.zeros_like(summed)])
        turned = jnp.concatenate([difference * cosine, difference * sine_value])
    else:
        turned = jnp.stack(
            [
                difference[0] * cosine - difference[1] * sine_value,
                difference[0] * sine_value + difference[1] * cosine,
            ]
        )
    return jnp.where(upper_half, turned, summed)


def local_table(k_first, slab_count, length):
    total = slab_count * length
    row_index = lax.broadcasted_iota(jnp.int32, (length, length), 0)
    col_index = lax.broadcasted_iota(jnp.int32, (length, length), 1)
    phase = col_index * (k_first + slab_count * row_index) % total
    phase_angle = phase.astype(jnp.float32) * (TWO_PI / total)
    return (jnp.cos(phase_angle), -jnp.sin(phase_angle))


def along(parts, table_real, table_imag, spec):
    def product(data, table):
        return jnp.einsum(
            spec,
            data,
            table,
            precision=lax.Precision.HIGHEST,
            preferred_element_type=jnp.float32,
        )

    return jnp.stack(
        [
            product(parts[0], table_real) - product(parts[1], table_imag),
            product(parts[0], table_imag) + product(parts[1], table_real),
        ]
    )


def dense_shards(
    resident_rows,
    resident_columns,
    resident_strength,
    crossing_rows,
    crossing_columns,
    crossing_strength,
    crossing_count,
):
    cells_x = NX // lax.axis_size("gx")
    cells_y = NY // lax.axis_size("gy")
    slot_count = crossing_rows.shape[-1]
    slot_index = lax.broadcasted_iota(jnp.int32, (1, slot_count), 1)
    live_slot = (slot_index < crossing_count).astype(jnp.float32)
    outgoing = jnp.concatenate(
        [
            crossing_rows.reshape(1, slot_count).astype(jnp.float32),
            crossing_columns.reshape(1, slot_count).astype(jnp.float32),
            crossing_strength.reshape(3, slot_count) * live_slot,
        ],
        axis=0,
    )
    arrived = from_behind(outgoing, "gx", 1)
    resident_ids = resident_rows.reshape(-1) * cells_x + resident_columns.reshape(-1)
    arrived_ids = arrived[0].astype(jnp.int32) * cells_x + arrived[1].astype(jnp.int32)
    cell_ids = jnp.concatenate([resident_ids, arrived_ids])
    weights = jnp.concatenate([resident_strength.reshape(3, -1), arrived[2:]], axis=1)
    cell_total = LEV * cells_y * cells_x
    deposited = jnp.stack(
        [
            jax.ops.segment_sum(weights[component], cell_ids, num_segments=cell_total)
            for component in range(3)
        ]
    )
    vorticity = deposited.reshape(1, 3, LEV, cells_y, cells_x) * (1.0 / math.sqrt(NX * NY))
    parts = vorticity
    for axis, cells, spec in (
        ("gx", cells_x, "clyx,kx->clyk"),
        ("gy", cells_y, "clyx,ky->clkx"),
    ):
        bits = lax.axis_size(axis).bit_length() - 1
        slab_index = lax.axis_index(axis)
        for bit_number in range(bits - 1, -1, -1):
            partner = partner_2(parts, axis, bit_number)
            parts = section_mix(parts, partner, slab_index, bit_number)
        table_real, table_imag = local_table(bit_reverse(slab_index, bits), 1 << bits, cells)
        parts = along(parts, table_real, table_imag, spec)
    return parts


def bin_key(rows, columns, cells_x):
    column = (columns & 1) * (cells_x // 2) + (columns >> 1)
    bin_index = (column // BIN_COLS) * 4 + (rows & 3)
    return bin_index * (BIN_ROWS * BIN_COLS) + (rows >> 2) * BIN_COLS + column % BIN_COLS


def deposit(sources, signs, cells_x, cells_y, base_mesh, after):
    count = len(sources)
    row_bins = cells_y // BIN_ROWS
    col_bins = cells_x // BIN_COLS
    width = sources[0].shape[-1]
    first_start = width - LANES
    window = CHUNK + LANES
    shift = BIN_COLS.bit_length() - 1
    based = base_mesh is not None

    def kernel(signs_ref, *refs):
        source_refs = refs[:count]
        base_ref = refs[count] if based else None
        out_ref, starts_ref, sems = refs[-3:]
        group = pl.program_id(0)

        @pl.when(group == 0)
        def _():
            copies = [
                pltpu.make_async_copy(
                    source_refs[s].at[pl.ds(0, 1), pl.ds(first_start, LANES)],
                    starts_ref.at[pl.ds(s, 1)],
                    sems.at[s],
                )
                for s in range(count)
            ]
            for copy in copies:
                copy.start()
            for copy in copies:
                copy.wait()

        spans = []
        steps = jnp.int32(0)
        for row_bin in range(row_bins):
            bin_index = group * row_bins + row_bin
            for s in range(count):
                begin = starts_ref[s, bin_index].astype(jnp.int32)
                end = starts_ref[s, bin_index + 1].astype(jnp.int32)
                spans.append((begin, end))
                steps = jnp.maximum(steps, (end - begin + CHUNK - 1) // CHUNK)
        lane = lax.broadcasted_iota(jnp.int32, (1, CHUNK), 1)

        def ramp(length):
            return (
                lax.broadcasted_iota(jnp.int32, (length, CHUNK), 0)
                .astype(jnp.float32)
                .astype(jnp.bfloat16)
            )

        row_ramp, col_ramp = ramp(BIN_ROWS), ramp(BIN_COLS)
        one, zero = jnp.bfloat16(1), jnp.bfloat16(0)

        def bin_total(step, row_bin):
            base = (group * row_bins + row_bin) * (BIN_ROWS * BIN_COLS)
            hits, weights = [], []
            for s in range(count):
                begin, end = spans[row_bin * count + s]
                here = jnp.minimum(begin + step * CHUNK, end)
                offset = jnp.minimum((here // LANES) * LANES, width - window)
                block = source_refs[s][:, pl.ds(pl.multiple_of(offset, LANES), window)]
                block = pltpu.roll(block, lax.rem(window - (here - offset), window), 1)[:, :CHUNK]
                local = block[0:1].astype(jnp.int32) - base
                row = jnp.where(
                    lane < end - here, lax.shift_right_arithmetic(local, shift), -1
                )
                col = local & (BIN_COLS - 1)
                row = row.astype(jnp.float32).astype(jnp.bfloat16)
                col = col.astype(jnp.float32).astype(jnp.bfloat16)
                hits.append(jnp.where(row_ramp == row, one, zero))
                mask = col_ramp == col
                weights.append(
                    jnp.concatenate(
                        [
                            jnp.where(
                                mask,
                                jnp.broadcast_to(piece[k : k + 1], (BIN_COLS, CHUNK)),
                                zero,
                            )
                            for piece in split(block * signs_ref[s])
                            for k in (1, 2, 3)
                        ],
                        axis=0,
                    )
                )
            total = lax.dot_general(
                jnp.concatenate(weights, axis=1),
                jnp.concatenate(hits, axis=1),
                (((1,), (1,)), ((), ())),
                preferred_element_type=jnp.float32,
            )
            total = total[: 3 * BIN_COLS] + total[3 * BIN_COLS :]
            return total.reshape(3, BIN_COLS, BIN_ROWS)

        def bin_rows(row_bin):
            return slice(row_bin * BIN_ROWS, (row_bin + 1) * BIN_ROWS)

        def body(step, carry):
            totals = [bin_total(step, row_bin) for row_bin in range(row_bins)]
            for row_bin in range(row_bins):
                out_ref[:, :, bin_rows(row_bin)] += totals[row_bin]
            return carry

        for row_bin in range(row_bins):
            total = bin_total(0, row_bin)
            where = bin_rows(row_bin)
            out_ref[:, :, where] = total + base_ref[:, :, where] if based else total
        lax.fori_loop(1, steps, body, 0)

    flops = count * width * BIN_ROWS * BIN_COLS * 24
    out_spec = pl.BlockSpec((3, BIN_COLS, cells_y), lambda g: (0, g, 0))
    return pl.pallas_call(
        kernel,
        grid=(col_bins,),
        in_specs=[pl.BlockSpec(memory_space=pltpu.SMEM)]
        + [pl.BlockSpec(memory_space=pltpu.VMEM)] * count
        + [out_spec] * based
        + [pl.BlockSpec(memory_space=pl.ANY)] * len(after),
        out_specs=out_spec,
        out_shape=jax.ShapeDtypeStruct((3, cells_x, cells_y), jnp.float32),
        scratch_shapes=[
            pltpu.SMEM((count, LANES), jnp.float32),
            pltpu.SemaphoreType.DMA((count,)),
        ],
        compiler_params=pltpu.CompilerParams(vmem_limit_bytes=14 << 20),
        cost_estimate=pl.CostEstimate(
            flops=flops, bytes_accessed=12 * cells_x * cells_y, transcendentals=0
        ),
        name="deposit",
    )(signs, *sources, *([base_mesh] if based else []), *after)


def turns(numerator, total):
    angle = (numerator % total).astype(jnp.float32) * (TWO_PI / total)
    return jnp.cos(angle), -jnp.sin(angle)


def stage_table(k_first, slab_count, radix, length):
    total = slab_count * radix * length
    shape = (radix, length, length)
    residue = lax.broadcasted_iota(jnp.int32, shape, 0)
    k = k_first + slab_count * lax.broadcasted_iota(jnp.int32, shape, 1)
    n = radix * lax.broadcasted_iota(jnp.int32, shape, 2) + residue
    real, imag = turns(k * n, total)
    return jnp.concatenate(
        [jnp.concatenate([real, -imag], axis=2), jnp.concatenate([imag, real], axis=2)], axis=1
    )


def split(value):
    high = value.astype(jnp.bfloat16)
    return high, (value - high.astype(jnp.float32)).astype(jnp.bfloat16)


def split_table(table):
    radix, length, _ = table.shape

    def kernel(table_ref, held_ref):
        high, low = split(table_ref[0])
        held_ref[0] = jnp.concatenate([high, high, low], axis=1)

    return pl.pallas_call(
        kernel,
        grid=(radix,),
        in_specs=[pl.BlockSpec((1, length, length), lambda g: (g, 0, 0))],
        out_specs=pl.BlockSpec((1, length, 3 * length), lambda g: (g, 0, 0)),
        out_shape=jax.ShapeDtypeStruct((radix, length, 3 * length), jnp.bfloat16),
        name="split_table",
    )(table)


def columns_transform(meshes, scalars, held, component, block):
    count = len(meshes)
    cells_x, cells_y = meshes[0].shape[1:]
    half = cells_x // 2

    def kernel(scalars_ref, held_ref, *refs):
        mesh_refs, out_ref = refs[:count], refs[count]
        pieces = []
        for residue in range(2):
            rows = slice(residue * half, (residue + 1) * half)
            data = [mesh_ref[0, rows, :] for mesh_ref in mesh_refs]
            real = sum(scalars_ref[0, i] * data[i] for i in range(count))
            imag = sum(scalars_ref[1, i] * data[i] for i in range(count))
            high, low = split(jnp.concatenate([real, imag], axis=0))
            pieces.append(
                jnp.dot(
                    held_ref[residue],
                    jnp.concatenate([high, low, high], axis=0),
                    preferred_element_type=jnp.float32,
                )
            )
        for part in range(2):
            rows = slice(part * half, (part + 1) * half)
            out_ref[part, 0, :half] = pieces[0][rows] + pieces[1][rows]
            out_ref[part, 0, half:] = pieces[0][rows] - pieces[1][rows]

    return pl.pallas_call(
        kernel,
        grid=(cells_y // block,),
        in_specs=[
            pl.BlockSpec(memory_space=pltpu.SMEM),
            pl.BlockSpec(memory_space=pltpu.VMEM),
        ]
        + [pl.BlockSpec((1, cells_x, block), lambda g: (component, 0, g))] * count,
        out_specs=pl.BlockSpec((2, 1, cells_x, block), lambda g: (0, 0, 0, g)),
        out_shape=jax.ShapeDtypeStruct((2, 1, cells_x, cells_y), jnp.float32),
        compiler_params=pltpu.CompilerParams(vmem_limit_bytes=20 << 20),
        cost_estimate=pl.CostEstimate(
            flops=12 * cells_x * cells_x * cells_y,
            bytes_accessed=(count + 2) * 4 * cells_x * cells_y,
            transcendentals=0,
        ),
        name="columns_transform",
    )(scalars, held, *meshes)


def rows_transform(own, partner, scalars, held, block, component, count, result):
    cells_x, cells_y = own.shape[2:]
    quarter = cells_y // 4

    def kernel(scalars_ref, held_ref, own_ref, partner_ref, *refs):
        out_ref = refs[-1]
        own_real, own_imag = scalars_ref[0], scalars_ref[1]
        other_real, other_imag = scalars_ref[2], scalars_ref[3]
        pieces = []
        for residue in range(4):
            where = slice(residue * quarter, (residue + 1) * quarter)
            a, b = own_ref[0, 0, :, where], own_ref[1, 0, :, where]
            d, e = partner_ref[0, 0, :, where], partner_ref[1, 0, :, where]
            real = own_real * a - own_imag * b + other_real * d - other_imag * e
            imag = own_real * b + own_imag * a + other_real * e + other_imag * d
            high, low = split(jnp.concatenate([real, imag], axis=1))
            piece = lax.dot_general(
                held_ref[residue],
                jnp.concatenate([high, low, high], axis=1),
                (((1,), (1,)), ((), ())),
                preferred_element_type=jnp.float32,
            )
            pieces.append((piece[:quarter], piece[quarter:]))
        (ar, ai), (br, bi), (cr, ci), (dr, di) = pieces
        even_r, even_i, odd_r, odd_i = ar + cr, ai + ci, br + dr, bi + di
        diff_r, diff_i, turn_r, turn_i = ar - cr, ai - ci, br - dr, bi - di
        out_ref[0, 0, 0, 0 * quarter : 1 * quarter] = even_r + odd_r
        out_ref[1, 0, 0, 0 * quarter : 1 * quarter] = even_i + odd_i
        out_ref[0, 0, 0, 1 * quarter : 2 * quarter] = diff_r + turn_i
        out_ref[1, 0, 0, 1 * quarter : 2 * quarter] = diff_i - turn_r
        out_ref[0, 0, 0, 2 * quarter : 3 * quarter] = even_r - odd_r
        out_ref[1, 0, 0, 2 * quarter : 3 * quarter] = even_i - odd_i
        out_ref[0, 0, 0, 3 * quarter : 4 * quarter] = diff_r - turn_i
        out_ref[1, 0, 0, 3 * quarter : 4 * quarter] = diff_i + turn_r

    spec = pl.BlockSpec((2, 1, block, cells_y), lambda g: (0, 0, g, 0))
    chained = result is not None
    return pl.pallas_call(
        kernel,
        grid=(cells_x // block,),
        in_specs=[
            pl.BlockSpec(memory_space=pltpu.SMEM),
            pl.BlockSpec(memory_space=pltpu.VMEM),
            spec,
            spec,
        ]
        + [pl.BlockSpec(memory_space=pl.ANY)] * chained,
        out_specs=pl.BlockSpec(
            (2, 1, 1, cells_y, block), lambda g: (0, component, 0, 0, g)
        ),
        out_shape=jax.ShapeDtypeStruct((2, count, 1, cells_y, cells_x), jnp.float32),
        input_output_aliases={4: 0} if chained else {},
        compiler_params=pltpu.CompilerParams(vmem_limit_bytes=32 << 20),
        cost_estimate=pl.CostEstimate(
            flops=6 * cells_y * cells_y * cells_x,
            bytes_accessed=24 * cells_x * cells_y,
            transcendentals=0,
        ),
        name="rows_transform",
    )(scalars, held, own, partner, *([result] if chained else []))


def particle_shards(
    resident_rows,
    resident_columns,
    resident_strength,
    crossing_rows,
    crossing_columns,
    crossing_strength,
    crossing_count,
):
    cells_x = NX // lax.axis_size("gx")
    cells_y = NY // lax.axis_size("gy")
    bins = (cells_y // BIN_ROWS) * (cells_x // BIN_COLS)
    gx, gy = lax.axis_index("gx"), lax.axis_index("gy")
    x, z = gx & 1, gx >> 1
    core, y = gy & 1, gy >> 1
    kx_first = bit_reverse(gx, 3)
    ky_first = bit_reverse(gy, 2)

    slot_count = crossing_rows.shape[-1]
    slot_index = lax.broadcasted_iota(jnp.int32, (1, slot_count), 1)
    live_slot = (slot_index < crossing_count).astype(jnp.float32)
    crossing_key = bin_key(crossing_rows.reshape(1, -1), crossing_columns.reshape(1, -1), cells_x)
    outgoing = jnp.concatenate(
        [crossing_key.astype(jnp.float32), crossing_strength.reshape(3, slot_count) * live_slot]
    )
    arrived = from_behind(outgoing, "gx", 1)
    resident_key = bin_key(resident_rows.reshape(-1), resident_columns.reshape(-1), cells_x)
    key = jnp.concatenate([resident_key, arrived[0].astype(jnp.int32)])
    strength = [
        jnp.concatenate([resident_strength[i].reshape(-1), arrived[1 + i]]) for i in range(3)
    ]
    key, *strength = lax.sort((key, *strength), num_keys=1, is_stable=False)
    bounds = lax.broadcasted_iota(jnp.int32, (LANES, 1), 0) * (BIN_ROWS * BIN_COLS)
    starts = jnp.sum((key[None, :] < bounds).astype(jnp.int32), axis=1)
    particles = jnp.concatenate(
        [
            jnp.stack([key.astype(jnp.float32), *strength]),
            jnp.concatenate([starts.astype(jnp.float32)[None], jnp.zeros((3, LANES), jnp.float32)]),
        ],
        axis=1,
    )

    held_x = split_table(stage_table(kx_first, 8, 2, cells_x // 2))
    held_y = split_table(stage_table(ky_first, 4, 4, cells_y // 4))

    kx_low = kx_first & 3

    def signs(slabs):
        values = []
        for k in slabs:
            for slab_y in (y, 1 - y):
                flips = kx_low * ((z ^ (k >> 1)) >> 1) + y * slab_y
                values.append((1 - 2 * (flips & 1)).astype(jnp.float32))
        return jnp.stack(values)

    near, far, meshes = {0: particles}, {}, {}
    last = [held_x, held_y]

    def add(*slabs):
        sources = [side[k] for k in slabs for side in (near, far)]
        kind = slabs[0] & 3
        meshes[kind] = deposit(
            sources, signs(slabs), cells_x, cells_y, meshes.get(kind), last[-2:]
        )
        last[:] = [meshes[kind]]

    def hold(*moved):
        held = lax.optimization_barrier([last[0]] + [side[k] for side, k in moved])
        last[0] = held[0]
        meshes[hold.kind] = held[0]
        for (side, k), value in zip(moved, held[1:]):
            side[k] = value

    far[0] = flip(near[0], "gy", 2)
    near[1] = flip(near[0], "gx", 1)
    near[4] = flip(near[0], "gx", 4)
    near[2] = flip(near[0], "gx", 2)
    far[1] = flip(near[1], "gy", 2)
    add(0)
    hold.kind = 0
    hold((near, 4), (near, 2))
    far[4] = flip(near[4], "gy", 2)
    near[5] = flip(near[4], "gx", 1)
    near[6] = flip(near[4], "gx", 2)
    far[2] = flip(near[2], "gy", 2)
    near[3] = flip(near[2], "gx", 1)
    add(1)
    hold.kind = 1
    hold((far, 4), (near, 5), (near, 6), (near, 3), (far, 2))
    far[5] = flip(far[4], "gx", 1)
    far[6] = flip(near[6], "gy", 2)
    near[7] = flip(near[6], "gx", 1)
    add(4)
    hold.kind = 0
    hold((near, 7), (near, 3))
    far[3] = flip(near[3], "gy", 2)
    far[7] = flip(near[7], "gy", 2)
    add(5)
    add(2, 6)
    add(3, 7)
    meshes = [meshes[kind] for kind in range(4)]
    scalars = []
    for kind in range(4):
        slab_x, slab_z = x ^ (kind & 1), (z ^ (kind >> 1)) & 1
        real, imag = turns(kx_first * slab_x + 2 * kx_low * slab_z, 8)
        scalars.append(jnp.stack([real, imag]) * (1.0 / math.sqrt(NX * NY)))
    scalars = jnp.stack(scalars, axis=1)

    owns = [columns_transform(meshes, scalars, held_x, i, 256) for i in range(3)]
    partners = [flip(own, "gy", 1) for own in owns]

    turn_real, turn_imag = turns(ky_first, 4)
    low = core == 0
    scalars = jnp.stack(
        [
            jnp.where(low, 1.0, turn_real),
            jnp.where(low, 0.0, turn_imag),
            jnp.where(low, turn_real, 1.0),
            jnp.where(low, turn_imag, 0.0),
        ]
    )
    result = None
    for i in range(3):
        result = rows_transform(owns[i], partners[i], scalars, held_y, 256, i, 3, result)
    return result


def solution(mesh):
    few = mesh.shape["gx"] == 8 and mesh.shape["gy"] == 4
    return jax.shard_map(
        particle_shards if few else dense_shards,
        mesh=mesh,
        in_specs=(
            P("gy", "gx", None),
            P("gy", "gx", None),
            P(None, "gy", "gx", None),
            P("gy", "gx", None),
            P("gy", "gx", None),
            P(None, "gy", "gx", None),
            P("gy", "gx"),
        ),
        out_specs=P(None, None, None, "gy", "gx"),
        check_vma=False,
    )
```

```python
import math

import jax
import jax.numpy as jnp
import ml_dtypes
import numpy as np
from jax import lax
from jax.experimental import pallas as pl
from jax.experimental.pallas import tpu as pltpu
from jax.sharding import PartitionSpec as P

NX = 4096
NY = 4096
LEV = 1


TWO_PI = 2.0 * math.pi

BIN_ROWS = 256
BIN_COLS = 32
CHUNK = 640
GROUP = 2
LANES = 128


def from_behind(value, axis, steps):
    count = lax.axis_size(axis)
    pairs = [(source, (source + steps) % count) for source in range(count)]
    return lax.ppermute(value, axis, pairs)


def flip(value, axis, mask):
    count = lax.axis_size(axis)
    return lax.ppermute(value, axis, [(source, source ^ mask) for source in range(count)])


def bit_reverse(slab_index, bit_count):
    result = jnp.zeros_like(slab_index)
    for level in range(bit_count):
        result = result | (slab_index >> level & 1) << bit_count - 1 - level
    return result


def partner_2(block, axis, stride):
    count = lax.axis_size(axis)
    route = []
    for low in range(count):
        high = low | 1 << stride
        if high != low and high < count:
            route += [(low, high), (high, low)]
    return lax.ppermute(block, axis, route)


def section_mix(parts, partner, slab_index, bit_number):
    half_span = 1 << bit_number
    upper_half = slab_index >> bit_number & 1 == 1
    phase_angle = (slab_index & half_span - 1).astype(jnp.float32) * (-math.pi / half_span)
    cosine = jnp.cos(phase_angle)
    sine_value = jnp.sin(phase_angle)
    summed = parts + partner
    difference = partner - parts
    if parts.shape[0] == 1:
        summed = jnp.concatenate([summed, jnp.zeros_like(summed)])
        turned = jnp.concatenate([difference * cosine, difference * sine_value])
    else:
        turned = jnp.stack(
            [
                difference[0] * cosine - difference[1] * sine_value,
                difference[0] * sine_value + difference[1] * cosine,
            ]
        )
    return jnp.where(upper_half, turned, summed)


def local_table(k_first, slab_count, length):
    total = slab_count * length
    row_index = lax.broadcasted_iota(jnp.int32, (length, length), 0)
    col_index = lax.broadcasted_iota(jnp.int32, (length, length), 1)
    phase = col_index * (k_first + slab_count * row_index) % total
    phase_angle = phase.astype(jnp.float32) * (TWO_PI / total)
    return (jnp.cos(phase_angle), -jnp.sin(phase_angle))


def along(parts, table_real, table_imag, spec):
    def product(data, table):
        return jnp.einsum(
            spec,
            data,
            table,
            precision=lax.Precision.HIGHEST,
            preferred_element_type=jnp.float32,
        )

    return jnp.stack(
        [
            product(parts[0], table_real) - product(parts[1], table_imag),
            product(parts[0], table_imag) + product(parts[1], table_real),
        ]
    )


def dense_shards(
    resident_rows,
    resident_columns,
    resident_strength,
    crossing_rows,
    crossing_columns,
    crossing_strength,
    crossing_count,
):
    cells_x = NX // lax.axis_size("gx")
    cells_y = NY // lax.axis_size("gy")
    slot_count = crossing_rows.shape[-1]
    slot_index = lax.broadcasted_iota(jnp.int32, (1, slot_count), 1)
    live_slot = (slot_index < crossing_count).astype(jnp.float32)
    outgoing = jnp.concatenate(
        [
            crossing_rows.reshape(1, slot_count).astype(jnp.float32),
            crossing_columns.reshape(1, slot_count).astype(jnp.float32),
            crossing_strength.reshape(3, slot_count) * live_slot,
        ],
        axis=0,
    )
    arrived = from_behind(outgoing, "gx", 1)
    resident_ids = resident_rows.reshape(-1) * cells_x + resident_columns.reshape(-1)
    arrived_ids = arrived[0].astype(jnp.int32) * cells_x + arrived[1].astype(jnp.int32)
    cell_ids = jnp.concatenate([resident_ids, arrived_ids])
    weights = jnp.concatenate([resident_strength.reshape(3, -1), arrived[2:]], axis=1)
    cell_total = LEV * cells_y * cells_x
    deposited = jnp.stack(
        [
            jax.ops.segment_sum(weights[component], cell_ids, num_segments=cell_total)
            for component in range(3)
        ]
    )
    vorticity = deposited.reshape(1, 3, LEV, cells_y, cells_x) * (1.0 / math.sqrt(NX * NY))
    parts = vorticity
    for axis, cells, spec in (
        ("gx", cells_x, "clyx,kx->clyk"),
        ("gy", cells_y, "clyx,ky->clkx"),
    ):
        bits = lax.axis_size(axis).bit_length() - 1
        slab_index = lax.axis_index(axis)
        for bit_number in range(bits - 1, -1, -1):
            partner = partner_2(parts, axis, bit_number)
            parts = section_mix(parts, partner, slab_index, bit_number)
        table_real, table_imag = local_table(bit_reverse(slab_index, bits), 1 << bits, cells)
        parts = along(parts, table_real, table_imag, spec)
    return parts


def bin_key(rows, columns, cells_x):
    column = (columns & 1) * (cells_x // 2) + (columns >> 1)
    bin_index = (column // BIN_COLS) * 4 + (rows & 3)
    return bin_index * (BIN_ROWS * BIN_COLS) + (rows >> 2) * BIN_COLS + column % BIN_COLS


def deposit(sources, signs, cells_x, cells_y, residents, base_mesh, after):
    count = len(sources)
    row_bins = cells_y // BIN_ROWS
    group_bins = row_bins * GROUP
    width = sources[0].shape[-1]
    first_start = width - LANES
    arrivals = first_start - residents
    window = CHUNK + LANES
    shift = BIN_COLS.bit_length() - 1
    based = base_mesh is not None

    def kernel(signs_ref, *refs):
        source_refs = refs[:count]
        base_ref = refs[count] if based else None
        out_ref, starts_ref, sems = refs[-3:]
        group = pl.program_id(0)

        @pl.when(group == 0)
        def _():
            copies = [
                pltpu.make_async_copy(
                    source_refs[s].at[pl.ds(0, 2), pl.ds(first_start, LANES)],
                    starts_ref.at[s],
                    sems.at[s],
                )
                for s in range(count)
            ]
            for copy in copies:
                copy.start()
            for copy in copies:
                copy.wait()

        spans = []
        steps = jnp.int32(0)
        for b in range(group_bins):
            bin_index = group * group_bins + b
            for s in range(count):
                begin, begin_2 = (starts_ref[s, i, bin_index].astype(jnp.int32) for i in (0, 1))
                end, end_2 = (starts_ref[s, i, bin_index + 1].astype(jnp.int32) for i in (0, 1))
                length, length_2 = end - begin, end_2 - begin_2
                spans.append((begin, length, begin_2, length_2))
                steps = jnp.maximum(steps, (length + length_2 + CHUNK - 1) // CHUNK)
                steps = jnp.maximum(steps, (length_2 + LANES - 1) // LANES)
        lane = lax.broadcasted_iota(jnp.int32, (1, CHUNK), 1)
        tail_lane = lax.broadcasted_iota(jnp.int32, (1, LANES), 1)

        def ramp(length):
            return (
                lax.broadcasted_iota(jnp.int32, (length, CHUNK), 0)
                .astype(jnp.float32)
                .astype(jnp.bfloat16)
            )

        row_ramp, col_ramp = ramp(BIN_ROWS), ramp(BIN_COLS)
        one, zero = jnp.bfloat16(1), jnp.bfloat16(0)

        def rolled(source_ref, place, low, high, size, lead):
            offset = low + jnp.minimum((place - low) // LANES * LANES, high - low - size)
            block = source_ref[:, pl.ds(pl.multiple_of(offset, LANES), size)]
            return pltpu.roll(block, lax.rem(2 * size + lead - (place - offset), size), 1)

        def bin_total(step, b):
            base = (group * group_bins + b) * (BIN_ROWS * BIN_COLS)
            hits, weights = [], []
            for s in range(count):
                begin, length, begin_2, length_2 = spans[b * count + s]
                done_2 = jnp.minimum(length_2, step * LANES)
                now_2 = jnp.minimum(length_2 - done_2, LANES)
                done = jnp.minimum(length, step * CHUNK - done_2)
                now = jnp.minimum(length - done, CHUNK - now_2)
                block = rolled(source_refs[s], begin + done, 0, residents, window, 0)[:, :CHUNK]
                tail = rolled(
                    source_refs[s],
                    residents + begin_2 + done_2,
                    residents,
                    residents + arrivals,
                    2 * LANES,
                    LANES - now_2,
                )[:, :LANES]
                tail = jnp.where(tail_lane >= LANES - now_2, tail, block[:, CHUNK - LANES :])
                block = jnp.concatenate([block[:, : CHUNK - LANES], tail], axis=1)
                local = block[0:1].astype(jnp.int32) - base
                row = jnp.where(
                    (lane < now) | (lane >= CHUNK - now_2),
                    lax.shift_right_arithmetic(local, shift),
                    -1,
                )
                col = local & (BIN_COLS - 1)
                row = row.astype(jnp.float32).astype(jnp.bfloat16)
                col = col.astype(jnp.float32).astype(jnp.bfloat16)
                hits.append(jnp.where(row_ramp == row, one, zero))
                mask = col_ramp == col
                weights.append(
                    jnp.concatenate(
                        [
                            jnp.where(
                                mask,
                                jnp.broadcast_to(piece[k : k + 1], (BIN_COLS, CHUNK)),
                                zero,
                            )
                            for piece in split(block * signs_ref[s])
                            for k in (1, 2, 3)
                        ],
                        axis=0,
                    )
                )
            total = lax.dot_general(
                jnp.concatenate(weights, axis=1),
                jnp.concatenate(hits, axis=1),
                (((1,), (1,)), ((), ())),
                preferred_element_type=jnp.float32,
            )
            total = total[: 3 * BIN_COLS] + total[3 * BIN_COLS :]
            return total.reshape(3, BIN_COLS, BIN_ROWS)

        def cells_of(b):
            col_bin, row_bin = b // row_bins, b % row_bins
            return (
                slice(None),
                slice(col_bin * BIN_COLS, (col_bin + 1) * BIN_COLS),
                slice(row_bin * BIN_ROWS, (row_bin + 1) * BIN_ROWS),
            )

        def body(step, carry):
            totals = [bin_total(step, b) for b in range(group_bins)]
            for b in range(group_bins):
                out_ref[cells_of(b)] += totals[b]
            return carry

        for b in range(group_bins):
            total = bin_total(0, b)
            out_ref[cells_of(b)] = total + base_ref[cells_of(b)] if based else total
        lax.fori_loop(1, steps, body, 0)

    flops = count * width * BIN_ROWS * BIN_COLS * 24
    out_spec = pl.BlockSpec((3, GROUP * BIN_COLS, cells_y), lambda g: (0, g, 0))
    return pl.pallas_call(
        kernel,
        grid=(cells_x // (GROUP * BIN_COLS),),
        in_specs=[pl.BlockSpec(memory_space=pltpu.SMEM)]
        + [pl.BlockSpec(memory_space=pltpu.VMEM)] * count
        + [out_spec] * based
        + [pl.BlockSpec(memory_space=pl.ANY)] * len(after),
        out_specs=out_spec,
        out_shape=jax.ShapeDtypeStruct((3, cells_x, cells_y), jnp.float32),
        scratch_shapes=[
            pltpu.SMEM((count, 2, LANES), jnp.float32),
            pltpu.SemaphoreType.DMA((count,)),
        ],
        compiler_params=pltpu.CompilerParams(vmem_limit_bytes=18 << 20),
        cost_estimate=pl.CostEstimate(
            flops=flops, bytes_accessed=12 * cells_x * cells_y, transcendentals=0
        ),
        name="deposit",
    )(signs, *sources, *([base_mesh] if based else []), *after)


def turns(numerator, total):
    angle = (numerator % total).astype(jnp.float32) * (TWO_PI / total)
    return jnp.cos(angle), -jnp.sin(angle)


def stage_table(radix, length):
    k = np.arange(length)[None, :, None]
    n = radix * np.arange(length)[None, None, :] + np.arange(radix)[:, None, None]
    angle = (k * n % (radix * length)) * (-TWO_PI / (radix * length))
    real, imag = np.cos(angle), np.sin(angle)
    table = np.concatenate(
        [np.concatenate([real, -imag], axis=2), np.concatenate([imag, real], axis=2)], axis=1
    )
    high = table.astype(ml_dtypes.bfloat16)
    low = (table - high.astype(np.float64)).astype(ml_dtypes.bfloat16)
    return jnp.asarray(np.concatenate([high, high, low], axis=2))


def phases(k_first, radix, length, total):
    place = lax.iota(jnp.int32, radix * length)
    return turns(k_first * (radix * (place % length) + place // length), total)


def split(value):
    high = value.astype(jnp.bfloat16)
    return high, (value - high.astype(jnp.float32)).astype(jnp.bfloat16)


def columns_transform(meshes, scalars, phase, held, component, block):
    count = len(meshes)
    cells_x, cells_y = meshes[0].shape[1:]
    half = cells_x // 2

    def kernel(scalars_ref, phase_ref, held_ref, *refs):
        mesh_refs, out_ref = refs[:count], refs[count]
        pieces = []
        for residue in range(2):
            rows = slice(residue * half, (residue + 1) * half)
            data = [mesh_ref[0, rows, :] for mesh_ref in mesh_refs]
            real = sum(scalars_ref[0, i] * data[i] for i in range(count))
            imag = sum(scalars_ref[1, i] * data[i] for i in range(count))
            cosine, sine = (
                jnp.concatenate([phase_ref[i, rows, :]] * (block // LANES), axis=1) for i in (0, 1)
            )
            real, imag = real * cosine - imag * sine, real * sine + imag * cosine
            high, low = split(jnp.concatenate([real, imag], axis=0))
            pieces.append(
                jnp.dot(
                    held_ref[residue],
                    jnp.concatenate([high, low, high], axis=0),
                    preferred_element_type=jnp.float32,
                )
            )
        for part in range(2):
            rows = slice(part * half, (part + 1) * half)
            out_ref[part, 0, :half] = pieces[0][rows] + pieces[1][rows]
            out_ref[part, 0, half:] = pieces[0][rows] - pieces[1][rows]

    return pl.pallas_call(
        kernel,
        grid=(cells_y // block,),
        in_specs=[
            pl.BlockSpec(memory_space=pltpu.SMEM),
            pl.BlockSpec(memory_space=pltpu.VMEM),
            pl.BlockSpec(memory_space=pltpu.VMEM),
        ]
        + [pl.BlockSpec((1, cells_x, block), lambda g: (component, 0, g))] * count,
        out_specs=pl.BlockSpec((2, 1, cells_x, block), lambda g: (0, 0, 0, g)),
        out_shape=jax.ShapeDtypeStruct((2, 1, cells_x, cells_y), jnp.float32),
        compiler_params=pltpu.CompilerParams(vmem_limit_bytes=20 << 20),
        cost_estimate=pl.CostEstimate(
            flops=12 * cells_x * cells_x * cells_y,
            bytes_accessed=(count + 2) * 4 * cells_x * cells_y,
            transcendentals=0,
        ),
        name="columns_transform",
    )(scalars, phase, held, *meshes)


def rows_transform(own, partner, scalars, held, block, component, count, result):
    cells_x, cells_y = own.shape[2:]
    quarter = cells_y // 4

    def kernel(scalars_ref, held_ref, own_ref, partner_ref, *refs):
        out_ref = refs[-1]
        pieces = []
        for residue in range(4):
            where = slice(residue * quarter, (residue + 1) * quarter)
            own_real, own_imag = scalars_ref[0:1, where], scalars_ref[1:2, where]
            other_real, other_imag = scalars_ref[2:3, where], scalars_ref[3:4, where]
            a, b = own_ref[0, 0, :, where], own_ref[1, 0, :, where]
            d, e = partner_ref[0, 0, :, where], partner_ref[1, 0, :, where]
            real = own_real * a - own_imag * b + other_real * d - other_imag * e
            imag = own_real * b + own_imag * a + other_real * e + other_imag * d
            high, low = split(jnp.concatenate([real, imag], axis=1))
            piece = lax.dot_general(
                held_ref[residue],
                jnp.concatenate([high, low, high], axis=1),
                (((1,), (1,)), ((), ())),
                preferred_element_type=jnp.float32,
            )
            pieces.append((piece[:quarter], piece[quarter:]))
        (ar, ai), (br, bi), (cr, ci), (dr, di) = pieces
        even_r, even_i, odd_r, odd_i = ar + cr, ai + ci, br + dr, bi + di
        diff_r, diff_i, turn_r, turn_i = ar - cr, ai - ci, br - dr, bi - di
        out_ref[0, 0, 0, 0 * quarter : 1 * quarter] = even_r + odd_r
        out_ref[1, 0, 0, 0 * quarter : 1 * quarter] = even_i + odd_i
        out_ref[0, 0, 0, 1 * quarter : 2 * quarter] = diff_r + turn_i
        out_ref[1, 0, 0, 1 * quarter : 2 * quarter] = diff_i - turn_r
        out_ref[0, 0, 0, 2 * quarter : 3 * quarter] = even_r - odd_r
        out_ref[1, 0, 0, 2 * quarter : 3 * quarter] = even_i - odd_i
        out_ref[0, 0, 0, 3 * quarter : 4 * quarter] = diff_r - turn_i
        out_ref[1, 0, 0, 3 * quarter : 4 * quarter] = diff_i + turn_r

    spec = pl.BlockSpec((2, 1, block, cells_y), lambda g: (0, 0, g, 0))
    chained = result is not None
    return pl.pallas_call(
        kernel,
        grid=(cells_x // block,),
        in_specs=[
            pl.BlockSpec(memory_space=pltpu.VMEM),
            pl.BlockSpec(memory_space=pltpu.VMEM),
            spec,
            spec,
        ]
        + [pl.BlockSpec(memory_space=pl.ANY)] * chained,
        out_specs=pl.BlockSpec(
            (2, 1, 1, cells_y, block), lambda g: (0, component, 0, 0, g)
        ),
        out_shape=jax.ShapeDtypeStruct((2, count, 1, cells_y, cells_x), jnp.float32),
        input_output_aliases={4: 0} if chained else {},
        compiler_params=pltpu.CompilerParams(vmem_limit_bytes=32 << 20),
        cost_estimate=pl.CostEstimate(
            flops=6 * cells_y * cells_y * cells_x,
            bytes_accessed=24 * cells_x * cells_y,
            transcendentals=0,
        ),
        name="rows_transform",
    )(scalars, held, own, partner, *([result] if chained else []))


def particle_shards(
    resident_rows,
    resident_columns,
    resident_strength,
    crossing_rows,
    crossing_columns,
    crossing_strength,
    crossing_count,
):
    cells_x = NX // lax.axis_size("gx")
    cells_y = NY // lax.axis_size("gy")
    bins = (cells_y // BIN_ROWS) * (cells_x // BIN_COLS)
    gx, gy = lax.axis_index("gx"), lax.axis_index("gy")
    x, z = gx & 1, gx >> 1
    core, y = gy & 1, gy >> 1
    kx_first = bit_reverse(gx, 3)
    ky_first = bit_reverse(gy, 2)

    bin_cells = BIN_ROWS * BIN_COLS
    slot_count = crossing_rows.shape[-1]
    live_slot = lax.iota(jnp.int32, slot_count) < crossing_count.reshape(1)
    key = bin_key(crossing_rows.reshape(-1), crossing_columns.reshape(-1), cells_x)
    key = jnp.where(live_slot, key, bins * bin_cells)
    outgoing = lax.sort(
        (key, *(jnp.where(live_slot, crossing_strength[i].reshape(-1), 0.0) for i in range(3))),
        num_keys=1,
        is_stable=False,
    )
    outgoing = jnp.stack([outgoing[0].astype(jnp.float32), *outgoing[1:]])
    arrived = from_behind(outgoing, "gx", 1)
    key = bin_key(resident_rows.reshape(-1), resident_columns.reshape(-1), cells_x)
    residents = key.shape[0]
    key, *strength = lax.sort(
        (key, *(resident_strength[i].reshape(-1) for i in range(3))), num_keys=1, is_stable=False
    )
    bounds = lax.broadcasted_iota(jnp.int32, (LANES, 1), 0) * bin_cells
    starts = jnp.sum((key[None, :] < bounds).astype(jnp.float32), axis=1)
    starts_2 = jnp.sum((arrived[0:1] < bounds.astype(jnp.float32)).astype(jnp.float32), axis=1)
    particles = jnp.concatenate(
        [
            jnp.stack([key.astype(jnp.float32), *strength]),
            arrived,
            jnp.stack([starts, starts_2, starts, starts]),
        ],
        axis=1,
    )

    held_x, held_y = stage_table(2, cells_x // 2), stage_table(4, cells_y // 4)
    kx_low = kx_first & 3

    def signs(slabs):
        values = []
        for k in slabs:
            for slab_y in (y, 1 - y):
                flips = kx_low * ((z ^ (k >> 1)) >> 1) + y * slab_y
                values.append((1 - 2 * (flips & 1)).astype(jnp.float32))
        return jnp.stack(values)

    near, far, meshes = {0: particles}, {}, {}
    last = []

    def add(*slabs):
        sources = [side[k] for k in slabs for side in (near, far)]
        kind = slabs[0] & 3
        meshes[kind] = deposit(
            sources, signs(slabs), cells_x, cells_y, residents, meshes.get(kind), last
        )
        last[:] = [meshes[kind]]

    def hold(*moved):
        held = lax.optimization_barrier([last[0]] + [side[k] for side, k in moved])
        last[0] = held[0]
        meshes[hold.kind] = held[0]
        for (side, k), value in zip(moved, held[1:]):
            side[k] = value

    far[0] = flip(near[0], "gy", 2)
    near[1] = flip(near[0], "gx", 1)
    near[4] = flip(near[0], "gx", 4)
    near[2] = flip(near[0], "gx", 2)
    far[1] = flip(near[1], "gy", 2)
    add(0)
    hold.kind = 0
    hold((near, 4), (near, 2))
    far[4] = flip(near[4], "gy", 2)
    near[5] = flip(near[4], "gx", 1)
    near[6] = flip(near[4], "gx", 2)
    far[2] = flip(near[2], "gy", 2)
    near[3] = flip(near[2], "gx", 1)
    add(1)
    hold.kind = 1
    hold((far, 4), (near, 5), (near, 6), (near, 3), (far, 2))
    far[5] = flip(far[4], "gx", 1)
    far[6] = flip(near[6], "gy", 2)
    near[7] = flip(near[6], "gx", 1)
    add(4)
    hold.kind = 0
    hold((near, 7), (near, 3))
    far[3] = flip(near[3], "gy", 2)
    far[7] = flip(near[7], "gy", 2)
    add(5)
    add(2, 6)
    add(3, 7)
    meshes = [meshes[kind] for kind in range(4)]
    scalars = []
    for kind in range(4):
        slab_x, slab_z = x ^ (kind & 1), (z ^ (kind >> 1)) & 1
        real, imag = turns(kx_first * slab_x + 2 * kx_low * slab_z, 8)
        scalars.append(jnp.stack([real, imag]) * (1.0 / math.sqrt(NX * NY)))
    scalars = jnp.stack(scalars, axis=1)

    phase = jnp.stack(phases(kx_first, 2, cells_x // 2, NX))
    phase = jnp.broadcast_to(phase[:, :, None], (2, cells_x, LANES))
    owns = [columns_transform(meshes, scalars, phase, held_x, i, 256) for i in range(3)]
    partners = [flip(own, "gy", 1) for own in owns]

    turn_real, turn_imag = turns(ky_first, 4)
    cosine, sine = phases(ky_first, 4, cells_y // 4, NY)
    with_turn = [cosine * turn_real - sine * turn_imag, cosine * turn_imag + sine * turn_real]
    own, other = jnp.stack([cosine, sine]), jnp.stack(with_turn)
    scalars = jnp.concatenate(
        [jnp.where(core == 0, own, other), jnp.where(core == 0, other, own)]
    )
    result = None
    for i in range(3):
        result = rows_transform(owns[i], partners[i], scalars, held_y, 256, i, 3, result)
    return result


def solution(mesh):
    few = mesh.shape["gx"] == 8 and mesh.shape["gy"] == 4
    return jax.shard_map(
        particle_shards if few else dense_shards,
        mesh=mesh,
        in_specs=(
            P("gy", "gx", None),
            P("gy", "gx", None),
            P(None, "gy", "gx", None),
            P("gy", "gx", None),
            P("gy", "gx", None),
            P(None, "gy", "gx", None),
            P("gy", "gx"),
        ),
        out_specs=P(None, None, None, "gy", "gx"),
        check_vma=False,
    )
```

```python
import math

import jax
import jax.numpy as jnp
import ml_dtypes
import numpy as np
from jax import lax
from jax.experimental import pallas as pl
from jax.experimental.pallas import tpu as pltpu
from jax.sharding import PartitionSpec as P

NX = 4096
NY = 4096
LEV = 1


TWO_PI = 2.0 * math.pi

BIN_ROWS = 256
BIN_COLS = 32
CHUNK = 640
GROUP = 2

F8 = jnp.float8_e4m3fn
PIECES = 3
STEP = 16.0
TOP = 384.0
LANES = 128


def from_behind(value, axis, steps):
    count = lax.axis_size(axis)
    pairs = [(source, (source + steps) % count) for source in range(count)]
    return lax.ppermute(value, axis, pairs)


def flip(value, axis, mask):
    count = lax.axis_size(axis)
    return lax.ppermute(value, axis, [(source, source ^ mask) for source in range(count)])


def bit_reverse(slab_index, bit_count):
    result = jnp.zeros_like(slab_index)
    for level in range(bit_count):
        result = result | (slab_index >> level & 1) << bit_count - 1 - level
    return result


def partner_2(block, axis, stride):
    count = lax.axis_size(axis)
    route = []
    for low in range(count):
        high = low | 1 << stride
        if high != low and high < count:
            route += [(low, high), (high, low)]
    return lax.ppermute(block, axis, route)


def section_mix(parts, partner, slab_index, bit_number):
    half_span = 1 << bit_number
    upper_half = slab_index >> bit_number & 1 == 1
    phase_angle = (slab_index & half_span - 1).astype(jnp.float32) * (-math.pi / half_span)
    cosine = jnp.cos(phase_angle)
    sine_value = jnp.sin(phase_angle)
    summed = parts + partner
    difference = partner - parts
    if parts.shape[0] == 1:
        summed = jnp.concatenate([summed, jnp.zeros_like(summed)])
        turned = jnp.concatenate([difference * cosine, difference * sine_value])
    else:
        turned = jnp.stack(
            [
                difference[0] * cosine - difference[1] * sine_value,
                difference[0] * sine_value + difference[1] * cosine,
            ]
        )
    return jnp.where(upper_half, turned, summed)


def local_table(k_first, slab_count, length):
    total = slab_count * length
    row_index = lax.broadcasted_iota(jnp.int32, (length, length), 0)
    col_index = lax.broadcasted_iota(jnp.int32, (length, length), 1)
    phase = col_index * (k_first + slab_count * row_index) % total
    phase_angle = phase.astype(jnp.float32) * (TWO_PI / total)
    return (jnp.cos(phase_angle), -jnp.sin(phase_angle))


def along(parts, table_real, table_imag, spec):
    def product(data, table):
        return jnp.einsum(
            spec,
            data,
            table,
            precision=lax.Precision.HIGHEST,
            preferred_element_type=jnp.float32,
        )

    return jnp.stack(
        [
            product(parts[0], table_real) - product(parts[1], table_imag),
            product(parts[0], table_imag) + product(parts[1], table_real),
        ]
    )


def dense_shards(
    resident_rows,
    resident_columns,
    resident_strength,
    crossing_rows,
    crossing_columns,
    crossing_strength,
    crossing_count,
):
    cells_x = NX // lax.axis_size("gx")
    cells_y = NY // lax.axis_size("gy")
    slot_count = crossing_rows.shape[-1]
    slot_index = lax.broadcasted_iota(jnp.int32, (1, slot_count), 1)
    live_slot = (slot_index < crossing_count).astype(jnp.float32)
    outgoing = jnp.concatenate(
        [
            crossing_rows.reshape(1, slot_count).astype(jnp.float32),
            crossing_columns.reshape(1, slot_count).astype(jnp.float32),
            crossing_strength.reshape(3, slot_count) * live_slot,
        ],
        axis=0,
    )
    arrived = from_behind(outgoing, "gx", 1)
    resident_ids = resident_rows.reshape(-1) * cells_x + resident_columns.reshape(-1)
    arrived_ids = arrived[0].astype(jnp.int32) * cells_x + arrived[1].astype(jnp.int32)
    cell_ids = jnp.concatenate([resident_ids, arrived_ids])
    weights = jnp.concatenate([resident_strength.reshape(3, -1), arrived[2:]], axis=1)
    cell_total = LEV * cells_y * cells_x
    deposited = jnp.stack(
        [
            jax.ops.segment_sum(weights[component], cell_ids, num_segments=cell_total)
            for component in range(3)
        ]
    )
    vorticity = deposited.reshape(1, 3, LEV, cells_y, cells_x) * (1.0 / math.sqrt(NX * NY))
    parts = vorticity
    for axis, cells, spec in (
        ("gx", cells_x, "clyx,kx->clyk"),
        ("gy", cells_y, "clyx,ky->clkx"),
    ):
        bits = lax.axis_size(axis).bit_length() - 1
        slab_index = lax.axis_index(axis)
        for bit_number in range(bits - 1, -1, -1):
            partner = partner_2(parts, axis, bit_number)
            parts = section_mix(parts, partner, slab_index, bit_number)
        table_real, table_imag = local_table(bit_reverse(slab_index, bits), 1 << bits, cells)
        parts = along(parts, table_real, table_imag, spec)
    return parts


def bin_key(rows, columns, cells_x):
    column = (columns & 1) * (cells_x // 2) + (columns >> 1)
    bin_index = (column // BIN_COLS) * 4 + (rows & 3)
    return bin_index * (BIN_ROWS * BIN_COLS) + (rows >> 2) * BIN_COLS + column % BIN_COLS


def deposit(sources, signs, cells_x, cells_y, residents, base_mesh, after):
    count = len(sources)
    row_bins = cells_y // BIN_ROWS
    group_bins = row_bins * GROUP
    width = sources[0].shape[-1]
    first_start = width - LANES
    arrivals = first_start - residents
    window = CHUNK + LANES
    shift = BIN_COLS.bit_length() - 1
    based = base_mesh is not None

    def kernel(signs_ref, *refs):
        source_refs = refs[:count]
        base_ref = refs[count] if based else None
        out_ref, starts_ref, sems = refs[-3:]
        group = pl.program_id(0)

        @pl.when(group == 0)
        def _():
            copies = [
                pltpu.make_async_copy(
                    source_refs[s].at[:, pl.ds(first_start, LANES)],
                    starts_ref.at[s],
                    sems.at[s],
                )
                for s in range(count)
            ]
            for copy in copies:
                copy.start()
            for copy in copies:
                copy.wait()

        scale, unscale = starts_ref[0, 2, 0], starts_ref[0, 3, 0]
        for s in range(1, count):
            scale = jnp.minimum(scale, starts_ref[s, 2, 0])
            unscale = jnp.maximum(unscale, starts_ref[s, 3, 0])
        spans = []
        steps = jnp.int32(0)
        for b in range(group_bins):
            bin_index = group * group_bins + b
            for s in range(count):
                begin, begin_2 = (starts_ref[s, i, bin_index].astype(jnp.int32) for i in (0, 1))
                end, end_2 = (starts_ref[s, i, bin_index + 1].astype(jnp.int32) for i in (0, 1))
                length, length_2 = end - begin, end_2 - begin_2
                spans.append((begin, length, begin_2, length_2))
                steps = jnp.maximum(steps, (length + length_2 + CHUNK - 1) // CHUNK)
                steps = jnp.maximum(steps, (length_2 + LANES - 1) // LANES)
        lane = lax.broadcasted_iota(jnp.int32, (1, CHUNK), 1)
        tail_lane = lax.broadcasted_iota(jnp.int32, (1, LANES), 1)

        def ramp(length):
            return (
                lax.broadcasted_iota(jnp.int32, (length, CHUNK), 0)
                .astype(jnp.float32)
                .astype(jnp.bfloat16)
            )

        row_ramp, col_ramp = ramp(BIN_ROWS), ramp(BIN_COLS)
        one, zero = jnp.bfloat16(1), jnp.bfloat16(0)

        def rolled(source_ref, place, low, high, size, lead):
            offset = low + jnp.minimum((place - low) // LANES * LANES, high - low - size)
            block = source_ref[:, pl.ds(pl.multiple_of(offset, LANES), size)]
            return pltpu.roll(block, lax.rem(2 * size + lead - (place - offset), size), 1)

        def bin_total(step, b):
            base = (group * group_bins + b) * (BIN_ROWS * BIN_COLS)
            hits, weights = [], []
            for s in range(count):
                begin, length, begin_2, length_2 = spans[b * count + s]
                done_2 = jnp.minimum(length_2, step * LANES)
                now_2 = jnp.minimum(length_2 - done_2, LANES)
                done = jnp.minimum(length, step * CHUNK - done_2)
                now = jnp.minimum(length - done, CHUNK - now_2)
                block = rolled(source_refs[s], begin + done, 0, residents, window, 0)[:, :CHUNK]
                tail = rolled(
                    source_refs[s],
                    residents + begin_2 + done_2,
                    residents,
                    residents + arrivals,
                    2 * LANES,
                    LANES - now_2,
                )[:, :LANES]
                tail = jnp.where(tail_lane >= LANES - now_2, tail, block[:, CHUNK - LANES :])
                block = jnp.concatenate([block[:, : CHUNK - LANES], tail], axis=1)
                local = block[0:1].astype(jnp.int32) - base
                row = jnp.where(
                    (lane < now) | (lane >= CHUNK - now_2),
                    lax.shift_right_arithmetic(local, shift),
                    -1,
                )
                col = local & (BIN_COLS - 1)
                row = row.astype(jnp.float32).astype(jnp.bfloat16)
                col = col.astype(jnp.float32).astype(jnp.bfloat16)
                hits.append(jnp.where(row_ramp == row, one, zero).astype(F8))
                mask = col_ramp == col
                pieces, rest = [], block * (signs_ref[s] * scale)
                for _ in range(PIECES):
                    piece = rest.astype(F8).astype(jnp.float32)
                    pieces.append(piece.astype(jnp.bfloat16))
                    rest = (rest - piece) * STEP
                weights.append(
                    jnp.concatenate(
                        [
                            jnp.where(
                                mask,
                                jnp.broadcast_to(piece[k : k + 1], (BIN_COLS, CHUNK)),
                                zero,
                            )
                            for piece in pieces
                            for k in (1, 2, 3)
                        ],
                        axis=0,
                    ).astype(F8)
                )
            total = lax.dot_general(
                jnp.concatenate(weights, axis=1),
                jnp.concatenate(hits, axis=1),
                (((1,), (1,)), ((), ())),
                preferred_element_type=jnp.float32,
            )
            total = total.reshape(PIECES, 3, BIN_COLS, BIN_ROWS)
            result = total[PIECES - 1]
            for piece in range(PIECES - 2, -1, -1):
                result = result * (1.0 / STEP) + total[piece]
            return result * unscale

        def cells_of(b):
            col_bin, row_bin = b // row_bins, b % row_bins
            return (
                slice(None),
                slice(col_bin * BIN_COLS, (col_bin + 1) * BIN_COLS),
                slice(row_bin * BIN_ROWS, (row_bin + 1) * BIN_ROWS),
            )

        def body(step, carry):
            totals = [bin_total(step, b) for b in range(group_bins)]
            for b in range(group_bins):
                out_ref[cells_of(b)] += totals[b]
            return carry

        for b in range(group_bins):
            total = bin_total(0, b)
            out_ref[cells_of(b)] = total + base_ref[cells_of(b)] if based else total
        lax.fori_loop(1, steps, body, 0)

    flops = count * width * BIN_ROWS * BIN_COLS * 24
    out_spec = pl.BlockSpec((3, GROUP * BIN_COLS, cells_y), lambda g: (0, g, 0))
    return pl.pallas_call(
        kernel,
        grid=(cells_x // (GROUP * BIN_COLS),),
        in_specs=[pl.BlockSpec(memory_space=pltpu.SMEM)]
        + [pl.BlockSpec(memory_space=pltpu.VMEM)] * count
        + [out_spec] * based
        + [pl.BlockSpec(memory_space=pl.ANY)] * len(after),
        out_specs=out_spec,
        out_shape=jax.ShapeDtypeStruct((3, cells_x, cells_y), jnp.float32),
        scratch_shapes=[
            pltpu.SMEM((count, 4, LANES), jnp.float32),
            pltpu.SemaphoreType.DMA((count,)),
        ],
        compiler_params=pltpu.CompilerParams(vmem_limit_bytes=10 << 20),
        cost_estimate=pl.CostEstimate(
            flops=flops, bytes_accessed=12 * cells_x * cells_y, transcendentals=0
        ),
        name="deposit",
    )(signs, *sources, *([base_mesh] if based else []), *after)


def turns(numerator, total):
    angle = (numerator % total).astype(jnp.float32) * (TWO_PI / total)
    return jnp.cos(angle), -jnp.sin(angle)


def stage_table(radix, length):
    k = np.arange(length)[None, :, None]
    n = radix * np.arange(length)[None, None, :] + np.arange(radix)[:, None, None]
    angle = (k * n % (radix * length)) * (-TWO_PI / (radix * length))
    real, imag = np.cos(angle), np.sin(angle)
    table = np.concatenate(
        [np.concatenate([real, -imag], axis=2), np.concatenate([imag, real], axis=2)], axis=1
    )
    high = table.astype(ml_dtypes.bfloat16)
    low = (table - high.astype(np.float64)).astype(ml_dtypes.bfloat16)
    return jnp.asarray(np.concatenate([high, high, low], axis=2))


def phases(k_first, radix, length, total):
    place = lax.iota(jnp.int32, radix * length)
    return turns(k_first * (radix * (place % length) + place // length), total)


def split(value):
    high = value.astype(jnp.bfloat16)
    return high, (value - high.astype(jnp.float32)).astype(jnp.bfloat16)


def columns_transform(meshes, scalars, phase, held, component, block):
    count = len(meshes)
    cells_x, cells_y = meshes[0].shape[1:]
    half = cells_x // 2

    def kernel(scalars_ref, phase_ref, held_ref, *refs):
        mesh_refs, out_ref = refs[:count], refs[count]
        lanes = pl.ds(pl.multiple_of(pl.program_id(0) * block, LANES), block)
        pieces = []
        for residue in range(2):
            rows = slice(residue * half, (residue + 1) * half)
            data = [mesh_ref[component, rows, lanes] for mesh_ref in mesh_refs]
            real = sum(scalars_ref[0, i] * data[i] for i in range(count))
            imag = sum(scalars_ref[1, i] * data[i] for i in range(count))
            cosine, sine = (
                jnp.concatenate([phase_ref[i, rows, :]] * (block // LANES), axis=1) for i in (0, 1)
            )
            real, imag = real * cosine - imag * sine, real * sine + imag * cosine
            high, low = split(jnp.concatenate([real, imag], axis=0))
            pieces.append(
                jnp.dot(
                    held_ref[residue],
                    jnp.concatenate([high, low, high], axis=0),
                    preferred_element_type=jnp.float32,
                )
            )
        for part in range(2):
            rows = slice(part * half, (part + 1) * half)
            out_ref[part, 0, :half] = pieces[0][rows] + pieces[1][rows]
            out_ref[part, 0, half:] = pieces[0][rows] - pieces[1][rows]

    return pl.pallas_call(
        kernel,
        grid=(cells_y // block,),
        in_specs=[
            pl.BlockSpec(memory_space=pltpu.SMEM),
            pl.BlockSpec(memory_space=pltpu.VMEM),
            pl.BlockSpec(memory_space=pltpu.VMEM),
        ]
        + [pl.BlockSpec(memory_space=pltpu.VMEM)] * count,
        out_specs=pl.BlockSpec((2, 1, cells_x, block), lambda g: (0, 0, 0, g)),
        out_shape=jax.ShapeDtypeStruct((2, 1, cells_x, cells_y), jnp.float32),
        compiler_params=pltpu.CompilerParams(vmem_limit_bytes=14 << 20),
        cost_estimate=pl.CostEstimate(
            flops=12 * cells_x * cells_x * cells_y,
            bytes_accessed=(count + 2) * 4 * cells_x * cells_y,
            transcendentals=0,
        ),
        name="columns_transform",
    )(scalars, phase, held, *meshes)


def rows_transform(own, partner, scalars, held, block, component, count, result):
    cells_x, cells_y = own.shape[2:]
    quarter = cells_y // 4

    def kernel(scalars_ref, held_ref, own_ref, partner_ref, *refs):
        out_ref = refs[-1]
        pieces = []
        for residue in range(4):
            where = slice(residue * quarter, (residue + 1) * quarter)
            own_real, own_imag = scalars_ref[0:1, where], scalars_ref[1:2, where]
            other_real, other_imag = scalars_ref[2:3, where], scalars_ref[3:4, where]
            a, b = own_ref[0, 0, :, where], own_ref[1, 0, :, where]
            d, e = partner_ref[0, 0, :, where], partner_ref[1, 0, :, where]
            real = own_real * a - own_imag * b + other_real * d - other_imag * e
            imag = own_real * b + own_imag * a + other_real * e + other_imag * d
            high, low = split(jnp.concatenate([real, imag], axis=1))
            piece = lax.dot_general(
                held_ref[residue],
                jnp.concatenate([high, low, high], axis=1),
                (((1,), (1,)), ((), ())),
                preferred_element_type=jnp.float32,
            )
            pieces.append((piece[:quarter], piece[quarter:]))
        (ar, ai), (br, bi), (cr, ci), (dr, di) = pieces
        even_r, even_i, odd_r, odd_i = ar + cr, ai + ci, br + dr, bi + di
        diff_r, diff_i, turn_r, turn_i = ar - cr, ai - ci, br - dr, bi - di
        out_ref[0, 0, 0, 0 * quarter : 1 * quarter] = even_r + odd_r
        out_ref[1, 0, 0, 0 * quarter : 1 * quarter] = even_i + odd_i
        out_ref[0, 0, 0, 1 * quarter : 2 * quarter] = diff_r + turn_i
        out_ref[1, 0, 0, 1 * quarter : 2 * quarter] = diff_i - turn_r
        out_ref[0, 0, 0, 2 * quarter : 3 * quarter] = even_r - odd_r
        out_ref[1, 0, 0, 2 * quarter : 3 * quarter] = even_i - odd_i
        out_ref[0, 0, 0, 3 * quarter : 4 * quarter] = diff_r - turn_i
        out_ref[1, 0, 0, 3 * quarter : 4 * quarter] = diff_i + turn_r

    spec = pl.BlockSpec((2, 1, block, cells_y), lambda g: (0, 0, g, 0))
    chained = result is not None
    return pl.pallas_call(
        kernel,
        grid=(cells_x // block,),
        in_specs=[
            pl.BlockSpec(memory_space=pltpu.VMEM),
            pl.BlockSpec(memory_space=pltpu.VMEM),
            spec,
            spec,
        ]
        + [pl.BlockSpec(memory_space=pl.ANY)] * chained,
        out_specs=pl.BlockSpec(
            (2, 1, 1, cells_y, block), lambda g: (0, component, 0, 0, g)
        ),
        out_shape=jax.ShapeDtypeStruct((2, count, 1, cells_y, cells_x), jnp.float32),
        input_output_aliases={4: 0} if chained else {},
        compiler_params=pltpu.CompilerParams(vmem_limit_bytes=24 << 20),
        cost_estimate=pl.CostEstimate(
            flops=6 * cells_y * cells_y * cells_x,
            bytes_accessed=24 * cells_x * cells_y,
            transcendentals=0,
        ),
        name="rows_transform",
    )(scalars, held, own, partner, *([result] if chained else []))


def particle_shards(
    resident_rows,
    resident_columns,
    resident_strength,
    crossing_rows,
    crossing_columns,
    crossing_strength,
    crossing_count,
):
    cells_x = NX // lax.axis_size("gx")
    cells_y = NY // lax.axis_size("gy")
    bins = (cells_y // BIN_ROWS) * (cells_x // BIN_COLS)
    gx, gy = lax.axis_index("gx"), lax.axis_index("gy")
    x, z = gx & 1, gx >> 1
    core, y = gy & 1, gy >> 1
    kx_first = bit_reverse(gx, 3)
    ky_first = bit_reverse(gy, 2)

    bin_cells = BIN_ROWS * BIN_COLS
    slot_count = crossing_rows.shape[-1]
    live_slot = lax.iota(jnp.int32, slot_count) < crossing_count.reshape(1)
    key = bin_key(crossing_rows.reshape(-1), crossing_columns.reshape(-1), cells_x)
    key = jnp.where(live_slot, key, bins * bin_cells)
    outgoing = lax.sort(
        (key, *(jnp.where(live_slot, crossing_strength[i].reshape(-1), 0.0) for i in range(3))),
        num_keys=1,
        is_stable=False,
    )
    outgoing = jnp.stack([outgoing[0].astype(jnp.float32), *outgoing[1:]])
    arrived = from_behind(outgoing, "gx", 1)
    key = bin_key(resident_rows.reshape(-1), resident_columns.reshape(-1), cells_x)
    residents = key.shape[0]
    key, *strength = lax.sort(
        (key, *(resident_strength[i].reshape(-1) for i in range(3))), num_keys=1, is_stable=False
    )
    bounds = lax.broadcasted_iota(jnp.int32, (LANES, 1), 0) * bin_cells
    starts = jnp.sum((key[None, :] < bounds).astype(jnp.float32), axis=1)
    starts_2 = jnp.sum((arrived[0:1] < bounds.astype(jnp.float32)).astype(jnp.float32), axis=1)
    largest = jnp.maximum(jnp.max(jnp.abs(resident_strength)), jnp.max(jnp.abs(arrived[1:])))
    largest = jnp.maximum(largest, 1e-30)
    particles = jnp.concatenate(
        [
            jnp.stack([key.astype(jnp.float32), *strength]),
            arrived,
            jnp.stack(
                [
                    starts,
                    starts_2,
                    jnp.broadcast_to(TOP / largest, (LANES,)),
                    jnp.broadcast_to(largest / TOP, (LANES,)),
                ]
            ),
        ],
        axis=1,
    )

    held_x, held_y = stage_table(2, cells_x // 2), stage_table(4, cells_y // 4)
    kx_low = kx_first & 3

    def signs(members):
        values = []
        for side, k in members:
            slab_y = y if side is near else 1 - y
            flips = kx_low * ((z ^ (k >> 1)) >> 1) + y * slab_y
            values.append((1 - 2 * (flips & 1)).astype(jnp.float32))
        return jnp.stack(values)

    near, far, meshes = {0: particles}, {}, {}
    last = []

    def add(*members):
        sources = [side[k] for side, k in members]
        kind = members[0][1] & 3
        meshes[kind] = deposit(
            sources, signs(members), cells_x, cells_y, residents, meshes.get(kind), last
        )
        last[:] = [meshes[kind]]
        hold.kind = kind

    def hold(*moved):
        held = lax.optimization_barrier([last[0]] + [side[k] for side, k in moved])
        last[0] = held[0]
        meshes[hold.kind] = held[0]
        for (side, k), value in zip(moved, held[1:]):
            side[k] = value

    far[0] = flip(near[0], "gy", 2)
    near[1] = flip(near[0], "gx", 1)
    near[4] = flip(near[0], "gx", 4)
    near[2] = flip(near[0], "gx", 2)
    add((near, 0))
    hold((near, 1))
    far[1] = flip(near[1], "gy", 2)
    add((far, 0))
    hold((near, 4), (near, 2))
    far[4] = flip(near[4], "gy", 2)
    near[5] = flip(near[4], "gx", 1)
    near[6] = flip(near[4], "gx", 2)
    far[2] = flip(near[2], "gy", 2)
    near[3] = flip(near[2], "gx", 1)
    add((near, 1), (far, 1))
    hold((far, 4), (near, 5), (near, 6), (near, 3), (far, 2))
    far[5] = flip(far[4], "gx", 1)
    far[6] = flip(near[6], "gy", 2)
    near[7] = flip(near[6], "gx", 1)
    add((near, 4), (far, 4))
    hold((near, 7), (near, 3))
    far[3] = flip(near[3], "gy", 2)
    far[7] = flip(near[7], "gy", 2)
    add((near, 5), (far, 5))
    add((near, 2), (far, 2), (near, 6), (far, 6))
    add((near, 3), (far, 3), (near, 7), (far, 7))
    meshes = [meshes[kind] for kind in range(4)]
    scalars = []
    for kind in range(4):
        slab_x, slab_z = x ^ (kind & 1), (z ^ (kind >> 1)) & 1
        real, imag = turns(kx_first * slab_x + 2 * kx_low * slab_z, 8)
        scalars.append(jnp.stack([real, imag]) * (1.0 / math.sqrt(NX * NY)))
    scalars = jnp.stack(scalars, axis=1)

    phase = jnp.stack(phases(kx_first, 2, cells_x // 2, NX))
    phase = jnp.broadcast_to(phase[:, :, None], (2, cells_x, LANES))
    owns = [columns_transform(meshes, scalars, phase, held_x, i, 256) for i in range(3)]
    partners = [flip(own, "gy", 1) for own in owns]

    turn_real, turn_imag = turns(ky_first, 4)
    cosine, sine = phases(ky_first, 4, cells_y // 4, NY)
    with_turn = [cosine * turn_real - sine * turn_imag, cosine * turn_imag + sine * turn_real]
    own, other = jnp.stack([cosine, sine]), jnp.stack(with_turn)
    scalars = jnp.concatenate(
        [jnp.where(core == 0, own, other), jnp.where(core == 0, other, own)]
    )
    result = None
    for i in range(3):
        result = rows_transform(owns[i], partners[i], scalars, held_y, 256, i, 3, result)
    return result


def solution(mesh):
    few = mesh.shape["gx"] == 8 and mesh.shape["gy"] == 4
    return jax.shard_map(
        particle_shards if few else dense_shards,
        mesh=mesh,
        in_specs=(
            P("gy", "gx", None),
            P("gy", "gx", None),
            P(None, "gy", "gx", None),
            P("gy", "gx", None),
            P("gy", "gx", None),
            P(None, "gy", "gx", None),
            P("gy", "gx"),
        ),
        out_specs=P(None, None, None, "gy", "gx"),
        check_vma=False,
    )
```

```python
import math

import jax
import jax.numpy as jnp
import ml_dtypes
import numpy as np
from jax import lax
from jax.experimental import pallas as pl
from jax.experimental.pallas import tpu as pltpu
from jax.sharding import PartitionSpec as P

NX = 4096
NY = 4096
LEV = 1


TWO_PI = 2.0 * math.pi

BIN_ROWS = 256
BIN_COLS = 32
CHUNK = 640
GROUP = 2

F8 = jnp.float8_e4m3fn
PIECES = 3
STEP = 16.0
TOP = 384.0
LANES = 128


def from_behind(value, axis, steps):
    count = lax.axis_size(axis)
    pairs = [(source, (source + steps) % count) for source in range(count)]
    return lax.ppermute(value, axis, pairs)


def flip(value, axis, mask):
    count = lax.axis_size(axis)
    return lax.ppermute(value, axis, [(source, source ^ mask) for source in range(count)])


def bit_reverse(slab_index, bit_count):
    result = jnp.zeros_like(slab_index)
    for level in range(bit_count):
        result = result | (slab_index >> level & 1) << bit_count - 1 - level
    return result


def partner_2(block, axis, stride):
    count = lax.axis_size(axis)
    route = []
    for low in range(count):
        high = low | 1 << stride
        if high != low and high < count:
            route += [(low, high), (high, low)]
    return lax.ppermute(block, axis, route)


def section_mix(parts, partner, slab_index, bit_number):
    half_span = 1 << bit_number
    upper_half = slab_index >> bit_number & 1 == 1
    phase_angle = (slab_index & half_span - 1).astype(jnp.float32) * (-math.pi / half_span)
    cosine = jnp.cos(phase_angle)
    sine_value = jnp.sin(phase_angle)
    summed = parts + partner
    difference = partner - parts
    if parts.shape[0] == 1:
        summed = jnp.concatenate([summed, jnp.zeros_like(summed)])
        turned = jnp.concatenate([difference * cosine, difference * sine_value])
    else:
        turned = jnp.stack(
            [
                difference[0] * cosine - difference[1] * sine_value,
                difference[0] * sine_value + difference[1] * cosine,
            ]
        )
    return jnp.where(upper_half, turned, summed)


def local_table(k_first, slab_count, length):
    total = slab_count * length
    row_index = lax.broadcasted_iota(jnp.int32, (length, length), 0)
    col_index = lax.broadcasted_iota(jnp.int32, (length, length), 1)
    phase = col_index * (k_first + slab_count * row_index) % total
    phase_angle = phase.astype(jnp.float32) * (TWO_PI / total)
    return (jnp.cos(phase_angle), -jnp.sin(phase_angle))


def along(parts, table_real, table_imag, spec):
    def product(data, table):
        return jnp.einsum(
            spec,
            data,
            table,
            precision=lax.Precision.HIGHEST,
            preferred_element_type=jnp.float32,
        )

    return jnp.stack(
        [
            product(parts[0], table_real) - product(parts[1], table_imag),
            product(parts[0], table_imag) + product(parts[1], table_real),
        ]
    )


def dense_shards(
    resident_rows,
    resident_columns,
    resident_strength,
    crossing_rows,
    crossing_columns,
    crossing_strength,
    crossing_count,
):
    cells_x = NX // lax.axis_size("gx")
    cells_y = NY // lax.axis_size("gy")
    slot_count = crossing_rows.shape[-1]
    slot_index = lax.broadcasted_iota(jnp.int32, (1, slot_count), 1)
    live_slot = (slot_index < crossing_count).astype(jnp.float32)
    outgoing = jnp.concatenate(
        [
            crossing_rows.reshape(1, slot_count).astype(jnp.float32),
            crossing_columns.reshape(1, slot_count).astype(jnp.float32),
            crossing_strength.reshape(3, slot_count) * live_slot,
        ],
        axis=0,
    )
    arrived = from_behind(outgoing, "gx", 1)
    resident_ids = resident_rows.reshape(-1) * cells_x + resident_columns.reshape(-1)
    arrived_ids = arrived[0].astype(jnp.int32) * cells_x + arrived[1].astype(jnp.int32)
    cell_ids = jnp.concatenate([resident_ids, arrived_ids])
    weights = jnp.concatenate([resident_strength.reshape(3, -1), arrived[2:]], axis=1)
    cell_total = LEV * cells_y * cells_x
    deposited = jnp.stack(
        [
            jax.ops.segment_sum(weights[component], cell_ids, num_segments=cell_total)
            for component in range(3)
        ]
    )
    vorticity = deposited.reshape(1, 3, LEV, cells_y, cells_x) * (1.0 / math.sqrt(NX * NY))
    parts = vorticity
    for axis, cells, spec in (
        ("gx", cells_x, "clyx,kx->clyk"),
        ("gy", cells_y, "clyx,ky->clkx"),
    ):
        bits = lax.axis_size(axis).bit_length() - 1
        slab_index = lax.axis_index(axis)
        for bit_number in range(bits - 1, -1, -1):
            partner = partner_2(parts, axis, bit_number)
            parts = section_mix(parts, partner, slab_index, bit_number)
        table_real, table_imag = local_table(bit_reverse(slab_index, bits), 1 << bits, cells)
        parts = along(parts, table_real, table_imag, spec)
    return parts


def bin_key(rows, columns, cells_x):
    column = (columns & 1) * (cells_x // 2) + (columns >> 1)
    bin_index = (column // BIN_COLS) * 4 + (rows & 3)
    return bin_index * (BIN_ROWS * BIN_COLS) + (rows >> 2) * BIN_COLS + column % BIN_COLS


def deposit(sources, signs, cells_x, cells_y, residents, base_mesh, after):
    count = len(sources)
    row_bins = cells_y // BIN_ROWS
    group_bins = row_bins * GROUP
    width = sources[0].shape[-1]
    first_start = width - LANES
    arrivals = first_start - residents
    window = CHUNK + LANES
    shift = BIN_COLS.bit_length() - 1
    based = base_mesh is not None

    def kernel(signs_ref, *refs):
        source_refs = refs[:count]
        base_ref = refs[count] if based else None
        out_ref, starts_ref, sems = refs[-3:]
        group = pl.program_id(0)

        @pl.when(group == 0)
        def _():
            copies = [
                pltpu.make_async_copy(
                    source_refs[s].at[:, pl.ds(first_start, LANES)],
                    starts_ref.at[s],
                    sems.at[s],
                )
                for s in range(count)
            ]
            for copy in copies:
                copy.start()
            for copy in copies:
                copy.wait()

        scale, unscale = starts_ref[0, 2, 0], starts_ref[0, 3, 0]
        for s in range(1, count):
            scale = jnp.minimum(scale, starts_ref[s, 2, 0])
            unscale = jnp.maximum(unscale, starts_ref[s, 3, 0])
        spans = []
        steps = jnp.int32(0)
        for b in range(group_bins):
            bin_index = group * group_bins + b
            for s in range(count):
                begin, begin_2 = (starts_ref[s, i, bin_index].astype(jnp.int32) for i in (0, 1))
                end, end_2 = (starts_ref[s, i, bin_index + 1].astype(jnp.int32) for i in (0, 1))
                length, length_2 = end - begin, end_2 - begin_2
                spans.append((begin, length, begin_2, length_2))
                steps = jnp.maximum(steps, (length + length_2 + CHUNK - 1) // CHUNK)
                steps = jnp.maximum(steps, (length_2 + LANES - 1) // LANES)
        lane = lax.broadcasted_iota(jnp.int32, (1, CHUNK), 1)
        tail_lane = lax.broadcasted_iota(jnp.int32, (1, LANES), 1)

        def ramp(length):
            return (
                lax.broadcasted_iota(jnp.int32, (length, CHUNK), 0)
                .astype(jnp.float32)
                .astype(jnp.bfloat16)
            )

        row_ramp, col_ramp = ramp(BIN_ROWS), ramp(BIN_COLS)
        one, zero = jnp.bfloat16(1), jnp.bfloat16(0)

        def rolled(source_ref, place, low, high, size, lead):
            offset = low + jnp.minimum((place - low) // LANES * LANES, high - low - size)
            block = source_ref[:, pl.ds(pl.multiple_of(offset, LANES), size)]
            return pltpu.roll(block, lax.rem(2 * size + lead - (place - offset), size), 1)

        def bin_total(step, b):
            base = (group * group_bins + b) * (BIN_ROWS * BIN_COLS)
            hits, weights = [], []
            for s in range(count):
                begin, length, begin_2, length_2 = spans[b * count + s]
                done_2 = jnp.minimum(length_2, step * LANES)
                now_2 = jnp.minimum(length_2 - done_2, LANES)
                done = jnp.minimum(length, step * CHUNK - done_2)
                now = jnp.minimum(length - done, CHUNK - now_2)
                block = rolled(source_refs[s], begin + done, 0, residents, window, 0)[:, :CHUNK]
                tail = rolled(
                    source_refs[s],
                    residents + begin_2 + done_2,
                    residents,
                    residents + arrivals,
                    2 * LANES,
                    LANES - now_2,
                )[:, :LANES]
                tail = jnp.where(tail_lane >= LANES - now_2, tail, block[:, CHUNK - LANES :])
                block = jnp.concatenate([block[:, : CHUNK - LANES], tail], axis=1)
                local = block[0:1].astype(jnp.int32) - base
                row = jnp.where(
                    (lane < now) | (lane >= CHUNK - now_2),
                    lax.shift_right_arithmetic(local, shift),
                    -1,
                )
                col = local & (BIN_COLS - 1)
                row = row.astype(jnp.float32).astype(jnp.bfloat16)
                col = col.astype(jnp.float32).astype(jnp.bfloat16)
                hits.append(jnp.where(row_ramp == row, one, zero).astype(F8))
                mask = col_ramp == col
                pieces, rest = [], block * (signs_ref[s] * scale)
                for _ in range(PIECES):
                    piece = rest.astype(F8).astype(jnp.float32)
                    pieces.append(piece.astype(jnp.bfloat16))
                    rest = (rest - piece) * STEP
                weights.append(
                    jnp.concatenate(
                        [
                            jnp.where(
                                mask,
                                jnp.broadcast_to(piece[k : k + 1], (BIN_COLS, CHUNK)),
                                zero,
                            )
                            for piece in pieces
                            for k in (1, 2, 3)
                        ],
                        axis=0,
                    ).astype(F8)
                )
            total = lax.dot_general(
                jnp.concatenate(weights, axis=1),
                jnp.concatenate(hits, axis=1),
                (((1,), (1,)), ((), ())),
                preferred_element_type=jnp.float32,
            )
            total = total.reshape(PIECES, 3, BIN_COLS, BIN_ROWS)
            result = total[PIECES - 1]
            for piece in range(PIECES - 2, -1, -1):
                result = result * (1.0 / STEP) + total[piece]
            return result * unscale

        def cells_of(b):
            col_bin, row_bin = b // row_bins, b % row_bins
            return (
                slice(None),
                slice(col_bin * BIN_COLS, (col_bin + 1) * BIN_COLS),
                slice(row_bin * BIN_ROWS, (row_bin + 1) * BIN_ROWS),
            )

        def body(step, carry):
            totals = [bin_total(step, b) for b in range(group_bins)]
            for b in range(group_bins):
                out_ref[cells_of(b)] += totals[b]
            return carry

        for b in range(group_bins):
            total = bin_total(0, b)
            out_ref[cells_of(b)] = total + base_ref[cells_of(b)] if based else total
        lax.fori_loop(1, steps, body, 0)

    flops = count * width * BIN_ROWS * BIN_COLS * 24
    out_spec = pl.BlockSpec((3, GROUP * BIN_COLS, cells_y), lambda g: (0, g, 0))
    return pl.pallas_call(
        kernel,
        grid=(cells_x // (GROUP * BIN_COLS),),
        in_specs=[pl.BlockSpec(memory_space=pltpu.SMEM)]
        + [pl.BlockSpec(memory_space=pltpu.VMEM)] * count
        + [out_spec] * based
        + [pl.BlockSpec(memory_space=pl.ANY)] * len(after),
        out_specs=out_spec,
        out_shape=jax.ShapeDtypeStruct((3, cells_x, cells_y), jnp.float32),
        scratch_shapes=[
            pltpu.SMEM((count, 4, LANES), jnp.float32),
            pltpu.SemaphoreType.DMA((count,)),
        ],
        compiler_params=pltpu.CompilerParams(vmem_limit_bytes=10 << 20),
        cost_estimate=pl.CostEstimate(
            flops=flops, bytes_accessed=12 * cells_x * cells_y, transcendentals=0
        ),
        name="deposit",
    )(signs, *sources, *([base_mesh] if based else []), *after)


def turns(numerator, total):
    angle = (numerator % total).astype(jnp.float32) * (TWO_PI / total)
    return jnp.cos(angle), -jnp.sin(angle)


def stage_table(radix, length):
    k = np.arange(length)[None, :, None]
    n = radix * np.arange(length)[None, None, :] + np.arange(radix)[:, None, None]
    angle = (k * n % (radix * length)) * (-TWO_PI / (radix * length))
    real, imag = np.cos(angle), np.sin(angle)
    table = np.concatenate(
        [np.concatenate([real, -imag], axis=2), np.concatenate([imag, real], axis=2)], axis=1
    )
    high = table.astype(ml_dtypes.bfloat16)
    low = (table - high.astype(np.float64)).astype(ml_dtypes.bfloat16)
    return jnp.asarray(np.concatenate([high, high, low], axis=2))


def phases(k_first, radix, length, total):
    place = lax.iota(jnp.int32, radix * length)
    return turns(k_first * (radix * (place % length) + place // length), total)


def split(value):
    high = value.astype(jnp.bfloat16)
    return high, (value - high.astype(jnp.float32)).astype(jnp.bfloat16)


def columns_transform(meshes, scalars, phase, held, component, block):
    count = len(meshes)
    cells_x, cells_y = meshes[0].shape[1:]
    half = cells_x // 2

    def kernel(scalars_ref, phase_ref, held_ref, *refs):
        mesh_refs, out_ref = refs[:count], refs[count]
        lanes = pl.ds(pl.multiple_of(pl.program_id(0) * block, LANES), block)
        pieces = []
        for residue in range(2):
            rows = slice(residue * half, (residue + 1) * half)
            data = [mesh_ref[component, rows, lanes] for mesh_ref in mesh_refs]
            real = sum(scalars_ref[0, i] * data[i] for i in range(count))
            imag = sum(scalars_ref[1, i] * data[i] for i in range(count))
            cosine, sine = (
                jnp.concatenate([phase_ref[i, rows, :]] * (block // LANES), axis=1) for i in (0, 1)
            )
            real, imag = real * cosine - imag * sine, real * sine + imag * cosine
            high, low = split(jnp.concatenate([real, imag], axis=0))
            pieces.append(
                jnp.dot(
                    held_ref[residue],
                    jnp.concatenate([high, low, high], axis=0),
                    preferred_element_type=jnp.float32,
                )
            )
        for part in range(2):
            rows = slice(part * half, (part + 1) * half)
            out_ref[part, 0, :half] = pieces[0][rows] + pieces[1][rows]
            out_ref[part, 0, half:] = pieces[0][rows] - pieces[1][rows]

    return pl.pallas_call(
        kernel,
        grid=(cells_y // block,),
        in_specs=[
            pl.BlockSpec(memory_space=pltpu.SMEM),
            pl.BlockSpec(memory_space=pltpu.VMEM),
            pl.BlockSpec(memory_space=pltpu.VMEM),
        ]
        + [pl.BlockSpec(memory_space=pltpu.VMEM)] * count,
        out_specs=pl.BlockSpec((2, 1, cells_x, block), lambda g: (0, 0, 0, g)),
        out_shape=jax.ShapeDtypeStruct((2, 1, cells_x, cells_y), jnp.float32),
        compiler_params=pltpu.CompilerParams(vmem_limit_bytes=12 << 20),
        cost_estimate=pl.CostEstimate(
            flops=12 * cells_x * cells_x * cells_y,
            bytes_accessed=(count + 2) * 4 * cells_x * cells_y,
            transcendentals=0,
        ),
        name="columns_transform",
    )(scalars, phase, held, *meshes)


def rows_transform(own, partner, scalars, held, block, component, count, result):
    cells_x, cells_y = own.shape[2:]
    quarter = cells_y // 4

    def kernel(scalars_ref, held_ref, own_ref, partner_ref, *refs):
        out_ref = refs[-1]
        pieces = []
        for residue in range(4):
            where = slice(residue * quarter, (residue + 1) * quarter)
            own_real, own_imag = scalars_ref[0:1, where], scalars_ref[1:2, where]
            other_real, other_imag = scalars_ref[2:3, where], scalars_ref[3:4, where]
            a, b = own_ref[0, 0, :, where], own_ref[1, 0, :, where]
            d, e = partner_ref[0, 0, :, where], partner_ref[1, 0, :, where]
            real = own_real * a - own_imag * b + other_real * d - other_imag * e
            imag = own_real * b + own_imag * a + other_real * e + other_imag * d
            high, low = split(jnp.concatenate([real, imag], axis=1))
            piece = lax.dot_general(
                held_ref[residue],
                jnp.concatenate([high, low, high], axis=1),
                (((1,), (1,)), ((), ())),
                preferred_element_type=jnp.float32,
            )
            pieces.append((piece[:quarter], piece[quarter:]))
        (ar, ai), (br, bi), (cr, ci), (dr, di) = pieces
        even_r, even_i, odd_r, odd_i = ar + cr, ai + ci, br + dr, bi + di
        diff_r, diff_i, turn_r, turn_i = ar - cr, ai - ci, br - dr, bi - di
        out_ref[0, 0, 0, 0 * quarter : 1 * quarter] = even_r + odd_r
        out_ref[1, 0, 0, 0 * quarter : 1 * quarter] = even_i + odd_i
        out_ref[0, 0, 0, 1 * quarter : 2 * quarter] = diff_r + turn_i
        out_ref[1, 0, 0, 1 * quarter : 2 * quarter] = diff_i - turn_r
        out_ref[0, 0, 0, 2 * quarter : 3 * quarter] = even_r - odd_r
        out_ref[1, 0, 0, 2 * quarter : 3 * quarter] = even_i - odd_i
        out_ref[0, 0, 0, 3 * quarter : 4 * quarter] = diff_r - turn_i
        out_ref[1, 0, 0, 3 * quarter : 4 * quarter] = diff_i + turn_r

    spec = pl.BlockSpec((2, 1, block, cells_y), lambda g: (0, 0, g, 0))
    chained = result is not None
    return pl.pallas_call(
        kernel,
        grid=(cells_x // block,),
        in_specs=[
            pl.BlockSpec(memory_space=pltpu.VMEM),
            pl.BlockSpec(memory_space=pltpu.VMEM),
            spec,
            spec,
        ]
        + [pl.BlockSpec(memory_space=pl.ANY)] * chained,
        out_specs=pl.BlockSpec(
            (2, 1, 1, cells_y, block), lambda g: (0, component, 0, 0, g)
        ),
        out_shape=jax.ShapeDtypeStruct((2, count, 1, cells_y, cells_x), jnp.float32),
        input_output_aliases={4: 0} if chained else {},
        compiler_params=pltpu.CompilerParams(vmem_limit_bytes=24 << 20),
        cost_estimate=pl.CostEstimate(
            flops=6 * cells_y * cells_y * cells_x,
            bytes_accessed=24 * cells_x * cells_y,
            transcendentals=0,
        ),
        name="rows_transform",
    )(scalars, held, own, partner, *([result] if chained else []))


def particle_shards(
    resident_rows,
    resident_columns,
    resident_strength,
    crossing_rows,
    crossing_columns,
    crossing_strength,
    crossing_count,
):
    cells_x = NX // lax.axis_size("gx")
    cells_y = NY // lax.axis_size("gy")
    bins = (cells_y // BIN_ROWS) * (cells_x // BIN_COLS)
    gx, gy = lax.axis_index("gx"), lax.axis_index("gy")
    x, z = gx & 1, gx >> 1
    core, y = gy & 1, gy >> 1
    kx_first = bit_reverse(gx, 3)
    ky_first = bit_reverse(gy, 2)

    bin_cells = BIN_ROWS * BIN_COLS
    slot_count = crossing_rows.shape[-1]
    live_slot = lax.iota(jnp.int32, slot_count) < crossing_count.reshape(1)
    key = bin_key(crossing_rows.reshape(-1), crossing_columns.reshape(-1), cells_x)
    key = jnp.where(live_slot, key, bins * bin_cells)
    outgoing = lax.sort(
        (key, *(jnp.where(live_slot, crossing_strength[i].reshape(-1), 0.0) for i in range(3))),
        num_keys=1,
        is_stable=False,
    )
    outgoing = jnp.stack([outgoing[0].astype(jnp.float32), *outgoing[1:]])
    arrived = from_behind(outgoing, "gx", 1)
    key = bin_key(resident_rows.reshape(-1), resident_columns.reshape(-1), cells_x)
    residents = key.shape[0]
    key, *strength = lax.sort(
        (key, *(resident_strength[i].reshape(-1) for i in range(3))), num_keys=1, is_stable=False
    )
    bounds = lax.broadcasted_iota(jnp.int32, (LANES, 1), 0) * bin_cells
    starts = jnp.sum((key[None, :] < bounds).astype(jnp.float32), axis=1)
    starts_2 = jnp.sum((arrived[0:1] < bounds.astype(jnp.float32)).astype(jnp.float32), axis=1)
    largest = jnp.maximum(jnp.max(jnp.abs(resident_strength)), jnp.max(jnp.abs(arrived[1:])))
    largest = jnp.maximum(largest, 1e-30)
    particles = jnp.concatenate(
        [
            jnp.stack([key.astype(jnp.float32), *strength]),
            arrived,
            jnp.stack(
                [
                    starts,
                    starts_2,
                    jnp.broadcast_to(TOP / largest, (LANES,)),
                    jnp.broadcast_to(largest / TOP, (LANES,)),
                ]
            ),
        ],
        axis=1,
    )

    held_x, held_y = stage_table(2, cells_x // 2), stage_table(4, cells_y // 4)
    kx_low = kx_first & 3

    def signs(members):
        values = []
        for side, k in members:
            slab_y = y if side is near else 1 - y
            flips = kx_low * ((z ^ (k >> 1)) >> 1) + y * slab_y
            values.append((1 - 2 * (flips & 1)).astype(jnp.float32))
        return jnp.stack(values)

    near, far, meshes = {0: particles}, {}, {}
    last = []

    def add(*members):
        sources = [side[k] for side, k in members]
        kind = members[0][1] & 3
        meshes[kind] = deposit(
            sources, signs(members), cells_x, cells_y, residents, meshes.get(kind), last
        )
        last[:] = [meshes[kind]]
        hold.kind = kind

    def hold(*moved):
        held = lax.optimization_barrier([last[0]] + [side[k] for side, k in moved])
        last[0] = held[0]
        meshes[hold.kind] = held[0]
        for (side, k), value in zip(moved, held[1:]):
            side[k] = value

    far[0] = flip(near[0], "gy", 2)
    near[1] = flip(near[0], "gx", 1)
    near[4] = flip(near[0], "gx", 4)
    near[2] = flip(near[0], "gx", 2)
    add((near, 0))
    hold((near, 1))
    far[1] = flip(near[1], "gy", 2)
    add((far, 0))
    hold((near, 4), (near, 2))
    far[4] = flip(near[4], "gy", 2)
    near[5] = flip(near[4], "gx", 1)
    near[6] = flip(near[4], "gx", 2)
    far[2] = flip(near[2], "gy", 2)
    near[3] = flip(near[1], "gx", 2)
    add((near, 1), (far, 1))
    hold((far, 4), (near, 6))
    far[5] = flip(far[4], "gx", 1)
    far[6] = flip(near[6], "gy", 2)
    add((near, 4), (far, 4))
    hold((near, 6), (near, 3))
    near[7] = flip(near[6], "gx", 1)
    far[3] = flip(near[3], "gy", 2)
    add((near, 5), (far, 5))
    hold((near, 7))
    far[7] = flip(near[7], "gy", 2)
    add((near, 2), (far, 2), (near, 6), (far, 6))
    add((near, 3), (far, 3), (near, 7), (far, 7))
    meshes = [meshes[kind] for kind in range(4)]
    scalars = []
    for kind in range(4):
        slab_x, slab_z = x ^ (kind & 1), (z ^ (kind >> 1)) & 1
        real, imag = turns(kx_first * slab_x + 2 * kx_low * slab_z, 8)
        scalars.append(jnp.stack([real, imag]) * (1.0 / math.sqrt(NX * NY)))
    scalars = jnp.stack(scalars, axis=1)

    phase = jnp.stack(phases(kx_first, 2, cells_x // 2, NX))
    phase = jnp.broadcast_to(phase[:, :, None], (2, cells_x, LANES))
    owns = [columns_transform(meshes, scalars, phase, held_x, i, 512) for i in range(3)]
    partners = [flip(own, "gy", 1) for own in owns]

    turn_real, turn_imag = turns(ky_first, 4)
    cosine, sine = phases(ky_first, 4, cells_y // 4, NY)
    with_turn = [cosine * turn_real - sine * turn_imag, cosine * turn_imag + sine * turn_real]
    own, other = jnp.stack([cosine, sine]), jnp.stack(with_turn)
    scalars = jnp.concatenate(
        [jnp.where(core == 0, own, other), jnp.where(core == 0, other, own)]
    )
    result = None
    for i in range(3):
        result = rows_transform(owns[i], partners[i], scalars, held_y, 256, i, 3, result)
    return result


def solution(mesh):
    few = mesh.shape["gx"] == 8 and mesh.shape["gy"] == 4
    return jax.shard_map(
        particle_shards if few else dense_shards,
        mesh=mesh,
        in_specs=(
            P("gy", "gx", None),
            P("gy", "gx", None),
            P(None, "gy", "gx", None),
            P("gy", "gx", None),
            P("gy", "gx", None),
            P(None, "gy", "gx", None),
            P("gy", "gx"),
        ),
        out_specs=P(None, None, None, "gy", "gx"),
        check_vma=False,
    )
```

```python
import math

import jax
import jax.numpy as jnp
import ml_dtypes
import numpy as np
from jax import lax
from jax.experimental import pallas as pl
from jax.experimental.pallas import tpu as pltpu
from jax.sharding import PartitionSpec as P

NX = 4096
NY = 4096
LEV = 1


TWO_PI = 2.0 * math.pi

BIN_ROWS = 256
BIN_COLS = 32
CHUNK = 640
GROUP = 2

F8 = jnp.float8_e4m3fn
PIECES = 3
STEP = 16.0
TOP = 384.0
LANES = 128


def from_behind(value, axis, steps):
    count = lax.axis_size(axis)
    pairs = [(source, (source + steps) % count) for source in range(count)]
    return lax.ppermute(value, axis, pairs)


def flip(value, axis, mask):
    count = lax.axis_size(axis)
    return lax.ppermute(value, axis, [(source, source ^ mask) for source in range(count)])


def bit_reverse(slab_index, bit_count):
    result = jnp.zeros_like(slab_index)
    for level in range(bit_count):
        result = result | (slab_index >> level & 1) << bit_count - 1 - level
    return result


def partner_2(block, axis, stride):
    count = lax.axis_size(axis)
    route = []
    for low in range(count):
        high = low | 1 << stride
        if high != low and high < count:
            route += [(low, high), (high, low)]
    return lax.ppermute(block, axis, route)


def section_mix(parts, partner, slab_index, bit_number):
    half_span = 1 << bit_number
    upper_half = slab_index >> bit_number & 1 == 1
    phase_angle = (slab_index & half_span - 1).astype(jnp.float32) * (-math.pi / half_span)
    cosine = jnp.cos(phase_angle)
    sine_value = jnp.sin(phase_angle)
    summed = parts + partner
    difference = partner - parts
    if parts.shape[0] == 1:
        summed = jnp.concatenate([summed, jnp.zeros_like(summed)])
        turned = jnp.concatenate([difference * cosine, difference * sine_value])
    else:
        turned = jnp.stack(
            [
                difference[0] * cosine - difference[1] * sine_value,
                difference[0] * sine_value + difference[1] * cosine,
            ]
        )
    return jnp.where(upper_half, turned, summed)


def local_table(k_first, slab_count, length):
    total = slab_count * length
    row_index = lax.broadcasted_iota(jnp.int32, (length, length), 0)
    col_index = lax.broadcasted_iota(jnp.int32, (length, length), 1)
    phase = col_index * (k_first + slab_count * row_index) % total
    phase_angle = phase.astype(jnp.float32) * (TWO_PI / total)
    return (jnp.cos(phase_angle), -jnp.sin(phase_angle))


def along(parts, table_real, table_imag, spec):
    def product(data, table):
        return jnp.einsum(
            spec,
            data,
            table,
            precision=lax.Precision.HIGHEST,
            preferred_element_type=jnp.float32,
        )

    return jnp.stack(
        [
            product(parts[0], table_real) - product(parts[1], table_imag),
            product(parts[0], table_imag) + product(parts[1], table_real),
        ]
    )


def dense_shards(
    resident_rows,
    resident_columns,
    resident_strength,
    crossing_rows,
    crossing_columns,
    crossing_strength,
    crossing_count,
):
    cells_x = NX // lax.axis_size("gx")
    cells_y = NY // lax.axis_size("gy")
    slot_count = crossing_rows.shape[-1]
    slot_index = lax.broadcasted_iota(jnp.int32, (1, slot_count), 1)
    live_slot = (slot_index < crossing_count).astype(jnp.float32)
    outgoing = jnp.concatenate(
        [
            crossing_rows.reshape(1, slot_count).astype(jnp.float32),
            crossing_columns.reshape(1, slot_count).astype(jnp.float32),
            crossing_strength.reshape(3, slot_count) * live_slot,
        ],
        axis=0,
    )
    arrived = from_behind(outgoing, "gx", 1)
    resident_ids = resident_rows.reshape(-1) * cells_x + resident_columns.reshape(-1)
    arrived_ids = arrived[0].astype(jnp.int32) * cells_x + arrived[1].astype(jnp.int32)
    cell_ids = jnp.concatenate([resident_ids, arrived_ids])
    weights = jnp.concatenate([resident_strength.reshape(3, -1), arrived[2:]], axis=1)
    cell_total = LEV * cells_y * cells_x
    deposited = jnp.stack(
        [
            jax.ops.segment_sum(weights[component], cell_ids, num_segments=cell_total)
            for component in range(3)
        ]
    )
    vorticity = deposited.reshape(1, 3, LEV, cells_y, cells_x) * (1.0 / math.sqrt(NX * NY))
    parts = vorticity
    for axis, cells, spec in (
        ("gx", cells_x, "clyx,kx->clyk"),
        ("gy", cells_y, "clyx,ky->clkx"),
    ):
        bits = lax.axis_size(axis).bit_length() - 1
        slab_index = lax.axis_index(axis)
        for bit_number in range(bits - 1, -1, -1):
            partner = partner_2(parts, axis, bit_number)
            parts = section_mix(parts, partner, slab_index, bit_number)
        table_real, table_imag = local_table(bit_reverse(slab_index, bits), 1 << bits, cells)
        parts = along(parts, table_real, table_imag, spec)
    return parts


def bin_key(rows, columns, cells_x):
    column = (columns & 1) * (cells_x // 2) + (columns >> 1)
    bin_index = (column // BIN_COLS) * 4 + (rows & 3)
    return bin_index * (BIN_ROWS * BIN_COLS) + (rows >> 2) * BIN_COLS + column % BIN_COLS


def deposit(sources, signs, cells_x, cells_y, residents, base_mesh, after):
    count = len(sources)
    row_bins = cells_y // BIN_ROWS
    column_bins = GROUP if count > 2 else 2 * GROUP
    group_bins = row_bins * column_bins
    width = sources[0].shape[-1]
    first_start = width - LANES
    arrivals = first_start - residents
    window = CHUNK + LANES
    shift = BIN_COLS.bit_length() - 1
    based = base_mesh is not None

    def kernel(signs_ref, *refs):
        source_refs = refs[:count]
        base_ref = refs[count] if based else None
        out_ref, starts_ref, sems = refs[-3:]
        group = pl.program_id(0)

        @pl.when(group == 0)
        def _():
            copies = [
                pltpu.make_async_copy(
                    source_refs[s].at[:, pl.ds(first_start, LANES)],
                    starts_ref.at[s],
                    sems.at[s],
                )
                for s in range(count)
            ]
            for copy in copies:
                copy.start()
            for copy in copies:
                copy.wait()

        scale, unscale = starts_ref[0, 2, 0], starts_ref[0, 3, 0]
        for s in range(1, count):
            scale = jnp.minimum(scale, starts_ref[s, 2, 0])
            unscale = jnp.maximum(unscale, starts_ref[s, 3, 0])
        spans = []
        steps = jnp.int32(0)
        for b in range(group_bins):
            bin_index = group * group_bins + b
            for s in range(count):
                begin, begin_2 = (starts_ref[s, i, bin_index].astype(jnp.int32) for i in (0, 1))
                end, end_2 = (starts_ref[s, i, bin_index + 1].astype(jnp.int32) for i in (0, 1))
                length, length_2 = end - begin, end_2 - begin_2
                spans.append((begin, length, begin_2, length_2))
                steps = jnp.maximum(steps, (length + length_2 + CHUNK - 1) // CHUNK)
                steps = jnp.maximum(steps, (length_2 + LANES - 1) // LANES)
        lane = lax.broadcasted_iota(jnp.int32, (1, CHUNK), 1)
        tail_lane = lax.broadcasted_iota(jnp.int32, (1, LANES), 1)

        def ramp(length):
            return (
                lax.broadcasted_iota(jnp.int32, (length, CHUNK), 0)
                .astype(jnp.float32)
                .astype(jnp.bfloat16)
            )

        row_ramp, col_ramp = ramp(BIN_ROWS), ramp(BIN_COLS)
        one, zero = jnp.bfloat16(1), jnp.bfloat16(0)

        def rolled(source_ref, place, low, high, size, lead):
            offset = low + jnp.minimum((place - low) // LANES * LANES, high - low - size)
            block = source_ref[:, pl.ds(pl.multiple_of(offset, LANES), size)]
            return pltpu.roll(block, lax.rem(2 * size + lead - (place - offset), size), 1)

        def bin_total(step, b):
            base = (group * group_bins + b) * (BIN_ROWS * BIN_COLS)
            hits, weights = [], []
            for s in range(count):
                begin, length, begin_2, length_2 = spans[b * count + s]
                done_2 = jnp.minimum(length_2, step * LANES)
                now_2 = jnp.minimum(length_2 - done_2, LANES)
                done = jnp.minimum(length, step * CHUNK - done_2)
                now = jnp.minimum(length - done, CHUNK - now_2)
                block = rolled(source_refs[s], begin + done, 0, residents, window, 0)[:, :CHUNK]
                tail = rolled(
                    source_refs[s],
                    residents + begin_2 + done_2,
                    residents,
                    residents + arrivals,
                    2 * LANES,
                    LANES - now_2,
                )[:, :LANES]
                tail = jnp.where(tail_lane >= LANES - now_2, tail, block[:, CHUNK - LANES :])
                block = jnp.concatenate([block[:, : CHUNK - LANES], tail], axis=1)
                local = block[0:1].astype(jnp.int32) - base
                row = jnp.where(
                    (lane < now) | (lane >= CHUNK - now_2),
                    lax.shift_right_arithmetic(local, shift),
                    -1,
                )
                col = local & (BIN_COLS - 1)
                row = row.astype(jnp.float32).astype(jnp.bfloat16)
                col = col.astype(jnp.float32).astype(jnp.bfloat16)
                hits.append(jnp.where(row_ramp == row, one, zero).astype(F8))
                mask = col_ramp == col
                pieces, rest = [], block * (signs_ref[s] * scale)
                for _ in range(PIECES):
                    piece = rest.astype(F8).astype(jnp.float32)
                    pieces.append(piece.astype(jnp.bfloat16))
                    rest = (rest - piece) * STEP
                weights.append(
                    jnp.concatenate(
                        [
                            jnp.where(
                                mask,
                                jnp.broadcast_to(piece[k : k + 1], (BIN_COLS, CHUNK)),
                                zero,
                            )
                            for piece in pieces
                            for k in (1, 2, 3)
                        ],
                        axis=0,
                    ).astype(F8)
                )
            total = lax.dot_general(
                jnp.concatenate(weights, axis=1),
                jnp.concatenate(hits, axis=1),
                (((1,), (1,)), ((), ())),
                preferred_element_type=jnp.float32,
            )
            total = total.reshape(PIECES, 3, BIN_COLS, BIN_ROWS)
            result = total[PIECES - 1]
            for piece in range(PIECES - 2, -1, -1):
                result = result * (1.0 / STEP) + total[piece]
            return result * unscale

        def cells_of(b):
            col_bin, row_bin = b // row_bins, b % row_bins
            return (
                slice(None),
                slice(col_bin * BIN_COLS, (col_bin + 1) * BIN_COLS),
                slice(row_bin * BIN_ROWS, (row_bin + 1) * BIN_ROWS),
            )

        def body(step, carry):
            totals = [bin_total(step, b) for b in range(group_bins)]
            for b in range(group_bins):
                out_ref[cells_of(b)] += totals[b]
            return carry

        for b in range(group_bins):
            total = bin_total(0, b)
            out_ref[cells_of(b)] = total + base_ref[cells_of(b)] if based else total
        lax.fori_loop(1, steps, body, 0)

    flops = count * width * BIN_ROWS * BIN_COLS * 24
    out_spec = pl.BlockSpec((3, column_bins * BIN_COLS, cells_y), lambda g: (0, g, 0))
    return pl.pallas_call(
        kernel,
        grid=(cells_x // (column_bins * BIN_COLS),),
        in_specs=[pl.BlockSpec(memory_space=pltpu.SMEM)]
        + [pl.BlockSpec(memory_space=pltpu.VMEM)] * count
        + [out_spec] * based
        + [pl.BlockSpec(memory_space=pl.ANY)] * len(after),
        out_specs=out_spec,
        out_shape=jax.ShapeDtypeStruct((3, cells_x, cells_y), jnp.float32),
        scratch_shapes=[
            pltpu.SMEM((count, 4, LANES), jnp.float32),
            pltpu.SemaphoreType.DMA((count,)),
        ],
        compiler_params=pltpu.CompilerParams(vmem_limit_bytes=12 << 20),
        cost_estimate=pl.CostEstimate(
            flops=flops, bytes_accessed=12 * cells_x * cells_y, transcendentals=0
        ),
        name="deposit",
    )(signs, *sources, *([base_mesh] if based else []), *after)


def turns(numerator, total):
    angle = (numerator % total).astype(jnp.float32) * (TWO_PI / total)
    return jnp.cos(angle), -jnp.sin(angle)


def stage_table(radix, length):
    k = np.arange(length)[None, :, None]
    n = radix * np.arange(length)[None, None, :] + np.arange(radix)[:, None, None]
    angle = (k * n % (radix * length)) * (-TWO_PI / (radix * length))
    real, imag = np.cos(angle), np.sin(angle)
    table = np.concatenate(
        [np.concatenate([real, -imag], axis=2), np.concatenate([imag, real], axis=2)], axis=1
    )
    high = table.astype(ml_dtypes.bfloat16)
    low = (table - high.astype(np.float64)).astype(ml_dtypes.bfloat16)
    return jnp.asarray(np.concatenate([high, low], axis=2))


def tripled(held_ref, residue):
    length = held_ref.shape[1]
    high = held_ref[residue, :, :length]
    return jnp.concatenate([high, high, held_ref[residue, :, length:]], axis=1)


def phases(k_first, radix, length, total):
    place = lax.iota(jnp.int32, radix * length)
    return turns(k_first * (radix * (place % length) + place // length), total)


def split(value):
    high = value.astype(jnp.bfloat16)
    return high, (value - high.astype(jnp.float32)).astype(jnp.bfloat16)


def columns_transform(meshes, scalars, phase, held, component, block):
    count = len(meshes)
    cells_x, cells_y = meshes[0].shape[1:]
    half = cells_x // 2

    def kernel(scalars_ref, phase_ref, held_ref, *refs):
        mesh_refs, out_ref = refs[:count], refs[count]
        lanes = pl.ds(pl.multiple_of(pl.program_id(0) * block, LANES), block)
        pieces = []
        for residue in range(2):
            rows = slice(residue * half, (residue + 1) * half)
            data = [mesh_ref[component, rows, lanes] for mesh_ref in mesh_refs]
            real = sum(scalars_ref[0, i] * data[i] for i in range(count))
            imag = sum(scalars_ref[1, i] * data[i] for i in range(count))
            cosine, sine = (
                jnp.concatenate([phase_ref[i, rows, :]] * (block // LANES), axis=1) for i in (0, 1)
            )
            real, imag = real * cosine - imag * sine, real * sine + imag * cosine
            high, low = split(jnp.concatenate([real, imag], axis=0))
            pieces.append(
                jnp.dot(
                    tripled(held_ref, residue),
                    jnp.concatenate([high, low, high], axis=0),
                    preferred_element_type=jnp.float32,
                )
            )
        for part in range(2):
            rows = slice(part * half, (part + 1) * half)
            out_ref[part, 0, :half] = pieces[0][rows] + pieces[1][rows]
            out_ref[part, 0, half:] = pieces[0][rows] - pieces[1][rows]

    return pl.pallas_call(
        kernel,
        grid=(cells_y // block,),
        in_specs=[
            pl.BlockSpec(memory_space=pltpu.SMEM),
            pl.BlockSpec(memory_space=pltpu.VMEM),
            pl.BlockSpec(memory_space=pltpu.VMEM),
        ]
        + [pl.BlockSpec(memory_space=pltpu.VMEM)] * count,
        out_specs=pl.BlockSpec((2, 1, cells_x, block), lambda g: (0, 0, 0, g)),
        out_shape=jax.ShapeDtypeStruct((2, 1, cells_x, cells_y), jnp.float32),
        compiler_params=pltpu.CompilerParams(vmem_limit_bytes=12 << 20),
        cost_estimate=pl.CostEstimate(
            flops=12 * cells_x * cells_x * cells_y,
            bytes_accessed=(count + 2) * 4 * cells_x * cells_y,
            transcendentals=0,
        ),
        name="columns_transform",
    )(scalars, phase, held, *meshes)


def rows_transform(own, partner, scalars, held, block, component, count, result):
    cells_x, cells_y = own.shape[2:]
    quarter = cells_y // 4

    def kernel(scalars_ref, held_ref, own_ref, partner_ref, *refs):
        out_ref = refs[-1]
        pieces = []
        for residue in range(4):
            where = slice(residue * quarter, (residue + 1) * quarter)
            own_real, own_imag = scalars_ref[0:1, where], scalars_ref[1:2, where]
            other_real, other_imag = scalars_ref[2:3, where], scalars_ref[3:4, where]
            a, b = own_ref[0, 0, :, where], own_ref[1, 0, :, where]
            d, e = partner_ref[0, 0, :, where], partner_ref[1, 0, :, where]
            real = own_real * a - own_imag * b + other_real * d - other_imag * e
            imag = own_real * b + own_imag * a + other_real * e + other_imag * d
            high, low = split(jnp.concatenate([real, imag], axis=1))
            piece = lax.dot_general(
                tripled(held_ref, residue),
                jnp.concatenate([high, low, high], axis=1),
                (((1,), (1,)), ((), ())),
                preferred_element_type=jnp.float32,
            )
            pieces.append((piece[:quarter], piece[quarter:]))
        (ar, ai), (br, bi), (cr, ci), (dr, di) = pieces
        even_r, even_i, odd_r, odd_i = ar + cr, ai + ci, br + dr, bi + di
        diff_r, diff_i, turn_r, turn_i = ar - cr, ai - ci, br - dr, bi - di
        out_ref[0, 0, 0, 0 * quarter : 1 * quarter] = even_r + odd_r
        out_ref[1, 0, 0, 0 * quarter : 1 * quarter] = even_i + odd_i
        out_ref[0, 0, 0, 1 * quarter : 2 * quarter] = diff_r + turn_i
        out_ref[1, 0, 0, 1 * quarter : 2 * quarter] = diff_i - turn_r
        out_ref[0, 0, 0, 2 * quarter : 3 * quarter] = even_r - odd_r
        out_ref[1, 0, 0, 2 * quarter : 3 * quarter] = even_i - odd_i
        out_ref[0, 0, 0, 3 * quarter : 4 * quarter] = diff_r - turn_i
        out_ref[1, 0, 0, 3 * quarter : 4 * quarter] = diff_i + turn_r

    spec = pl.BlockSpec((2, 1, block, cells_y), lambda g: (0, 0, g, 0))
    chained = result is not None
    return pl.pallas_call(
        kernel,
        grid=(cells_x // block,),
        in_specs=[
            pl.BlockSpec(memory_space=pltpu.VMEM),
            pl.BlockSpec(memory_space=pltpu.VMEM),
            spec,
            spec,
        ]
        + [pl.BlockSpec(memory_space=pl.ANY)] * chained,
        out_specs=pl.BlockSpec(
            (2, 1, 1, cells_y, block), lambda g: (0, component, 0, 0, g)
        ),
        out_shape=jax.ShapeDtypeStruct((2, count, 1, cells_y, cells_x), jnp.float32),
        input_output_aliases={4: 0} if chained else {},
        compiler_params=pltpu.CompilerParams(vmem_limit_bytes=24 << 20),
        cost_estimate=pl.CostEstimate(
            flops=6 * cells_y * cells_y * cells_x,
            bytes_accessed=24 * cells_x * cells_y,
            transcendentals=0,
        ),
        name="rows_transform",
    )(scalars, held, own, partner, *([result] if chained else []))


def particle_shards(
    resident_rows,
    resident_columns,
    resident_strength,
    crossing_rows,
    crossing_columns,
    crossing_strength,
    crossing_count,
):
    cells_x = NX // lax.axis_size("gx")
    cells_y = NY // lax.axis_size("gy")
    bins = (cells_y // BIN_ROWS) * (cells_x // BIN_COLS)
    gx, gy = lax.axis_index("gx"), lax.axis_index("gy")
    x, z = gx & 1, gx >> 1
    core, y = gy & 1, gy >> 1
    kx_first = bit_reverse(gx, 3)
    ky_first = bit_reverse(gy, 2)

    bin_cells = BIN_ROWS * BIN_COLS
    slot_count = crossing_rows.shape[-1]
    live_slot = lax.iota(jnp.int32, slot_count) < crossing_count.reshape(1)
    key = bin_key(crossing_rows, crossing_columns, cells_x).reshape(-1)
    key = jnp.where(live_slot, key, bins * bin_cells)
    outgoing = lax.sort(
        (key, *(jnp.where(live_slot, crossing_strength[i].reshape(-1), 0.0) for i in range(3))),
        num_keys=1,
        is_stable=False,
    )
    outgoing = jnp.stack([outgoing[0].astype(jnp.float32), *outgoing[1:]])
    arrived = from_behind(outgoing, "gx", 1)
    key = bin_key(resident_rows, resident_columns, cells_x).reshape(-1)
    residents = key.shape[0]
    key, *strength = lax.sort(
        (key, *(resident_strength[i].reshape(-1) for i in range(3))), num_keys=1, is_stable=False
    )
    bounds = lax.broadcasted_iota(jnp.int32, (bins + 8, 1), 0) * bin_cells
    starts = jnp.sum((key[None, :] < bounds).astype(jnp.float32), axis=1)
    starts_2 = jnp.sum((arrived[0:1] < bounds.astype(jnp.float32)).astype(jnp.float32), axis=1)
    starts, starts_2 = (jnp.pad(values, (0, LANES - bins - 8)) for values in (starts, starts_2))
    largest = jnp.maximum(jnp.abs(strength[0]), jnp.abs(strength[1]))
    largest = jnp.max(jnp.maximum(largest, jnp.abs(strength[2])))
    largest = jnp.maximum(jnp.maximum(largest, jnp.max(jnp.abs(arrived[1:]))), 1e-30)
    particles = jnp.concatenate(
        [
            jnp.stack([key.astype(jnp.float32), *strength]),
            arrived,
            jnp.stack(
                [
                    starts,
                    starts_2,
                    jnp.broadcast_to(TOP / largest, (LANES,)),
                    jnp.broadcast_to(largest / TOP, (LANES,)),
                ]
            ),
        ],
        axis=1,
    )

    held_x, held_y = stage_table(2, cells_x // 2), stage_table(4, cells_y // 4)
    kx_low = kx_first & 3

    def signs(members):
        values = []
        for side, k in members:
            slab_y = y if side is near else 1 - y
            flips = kx_low * ((z ^ (k >> 1)) >> 1) + y * slab_y
            values.append((1 - 2 * (flips & 1)).astype(jnp.float32))
        return jnp.stack(values)

    near, far, meshes = {0: particles}, {}, {}
    last = []

    def add(*members):
        sources = [side[k] for side, k in members]
        kind = members[0][1] & 3
        meshes[kind] = deposit(
            sources, signs(members), cells_x, cells_y, residents, meshes.get(kind), last
        )
        last[:] = [meshes[kind]]
        hold.kind = kind

    def hold(*moved):
        held = lax.optimization_barrier([last[0]] + [side[k] for side, k in moved])
        last[0] = held[0]
        meshes[hold.kind] = held[0]
        for (side, k), value in zip(moved, held[1:]):
            side[k] = value

    far[0] = flip(near[0], "gy", 2)
    near[1] = flip(near[0], "gx", 1)
    near[4] = flip(near[0], "gx", 4)
    near[2] = flip(near[0], "gx", 2)
    add((near, 0))
    hold((near, 1))
    far[1] = flip(near[1], "gy", 2)
    add((far, 0))
    hold((near, 4), (near, 2))
    far[4] = flip(near[4], "gy", 2)
    near[5] = flip(near[4], "gx", 1)
    near[6] = flip(near[4], "gx", 2)
    far[2] = flip(near[2], "gy", 2)
    near[3] = flip(near[1], "gx", 2)
    add((near, 1), (far, 1))
    hold((far, 4), (near, 6))
    far[5] = flip(far[4], "gx", 1)
    far[6] = flip(near[6], "gy", 2)
    add((near, 4), (far, 4))
    hold((near, 6), (near, 3))
    near[7] = flip(near[6], "gx", 1)
    far[3] = flip(near[3], "gy", 2)
    add((near, 5), (far, 5))
    hold((near, 7))
    far[7] = flip(near[7], "gy", 2)
    add((near, 2), (far, 2), (near, 6), (far, 6))
    add((near, 3), (far, 3), (near, 7), (far, 7))
    meshes = [meshes[kind] for kind in range(4)]
    scalars = []
    for kind in range(4):
        slab_x, slab_z = x ^ (kind & 1), (z ^ (kind >> 1)) & 1
        real, imag = turns(kx_first * slab_x + 2 * kx_low * slab_z, 8)
        scalars.append(jnp.stack([real, imag]) * (1.0 / math.sqrt(NX * NY)))
    scalars = jnp.stack(scalars, axis=1)

    phase = jnp.stack(phases(kx_first, 2, cells_x // 2, NX))
    phase = jnp.broadcast_to(phase[:, :, None], (2, cells_x, LANES))
    owns = [columns_transform(meshes, scalars, phase, held_x, i, 512) for i in range(3)]
    partners = [flip(own, "gy", 1) for own in owns]

    turn_real, turn_imag = turns(ky_first, 4)
    cosine, sine = phases(ky_first, 4, cells_y // 4, NY)
    with_turn = [cosine * turn_real - sine * turn_imag, cosine * turn_imag + sine * turn_real]
    own, other = jnp.stack([cosine, sine]), jnp.stack(with_turn)
    scalars = jnp.concatenate(
        [jnp.where(core == 0, own, other), jnp.where(core == 0, other, own)]
    )
    result = None
    for i in range(3):
        result = rows_transform(owns[i], partners[i], scalars, held_y, 256, i, 3, result)
    return result


def solution(mesh):
    few = mesh.shape["gx"] == 8 and mesh.shape["gy"] == 4
    return jax.shard_map(
        particle_shards if few else dense_shards,
        mesh=mesh,
        in_specs=(
            P("gy", "gx", None),
            P("gy", "gx", None),
            P(None, "gy", "gx", None),
            P("gy", "gx", None),
            P("gy", "gx", None),
            P(None, "gy", "gx", None),
            P("gy", "gx"),
        ),
        out_specs=P(None, None, None, "gy", "gx"),
        check_vma=False,
    )
```

```python
import math

import jax
import jax.numpy as jnp
import ml_dtypes
import numpy as np
from jax import lax
from jax.experimental import pallas as pl
from jax.experimental.pallas import tpu as pltpu
from jax.sharding import PartitionSpec as P

NX = 4096
NY = 4096
LEV = 1


TWO_PI = 2.0 * math.pi

BIN_ROWS = 256
BIN_COLS = 32
CHUNK = 640
GROUP = 4

F8 = jnp.float8_e4m3fn
PIECES = 3
STEP = 16.0
TOP = 384.0
LANES = 128


def from_behind(value, axis, steps):
    count = lax.axis_size(axis)
    pairs = [(source, (source + steps) % count) for source in range(count)]
    return lax.ppermute(value, axis, pairs)


def flip(value, axis, mask):
    count = lax.axis_size(axis)
    return lax.ppermute(value, axis, [(source, source ^ mask) for source in range(count)])


def bit_reverse(slab_index, bit_count):
    result = jnp.zeros_like(slab_index)
    for level in range(bit_count):
        result = result | (slab_index >> level & 1) << bit_count - 1 - level
    return result


def partner_2(block, axis, stride):
    count = lax.axis_size(axis)
    route = []
    for low in range(count):
        high = low | 1 << stride
        if high != low and high < count:
            route += [(low, high), (high, low)]
    return lax.ppermute(block, axis, route)


def section_mix(parts, partner, slab_index, bit_number):
    half_span = 1 << bit_number
    upper_half = slab_index >> bit_number & 1 == 1
    phase_angle = (slab_index & half_span - 1).astype(jnp.float32) * (-math.pi / half_span)
    cosine = jnp.cos(phase_angle)
    sine_value = jnp.sin(phase_angle)
    summed = parts + partner
    difference = partner - parts
    if parts.shape[0] == 1:
        summed = jnp.concatenate([summed, jnp.zeros_like(summed)])
        turned = jnp.concatenate([difference * cosine, difference * sine_value])
    else:
        turned = jnp.stack(
            [
                difference[0] * cosine - difference[1] * sine_value,
                difference[0] * sine_value + difference[1] * cosine,
            ]
        )
    return jnp.where(upper_half, turned, summed)


def local_table(k_first, slab_count, length):
    total = slab_count * length
    row_index = lax.broadcasted_iota(jnp.int32, (length, length), 0)
    col_index = lax.broadcasted_iota(jnp.int32, (length, length), 1)
    phase = col_index * (k_first + slab_count * row_index) % total
    phase_angle = phase.astype(jnp.float32) * (TWO_PI / total)
    return (jnp.cos(phase_angle), -jnp.sin(phase_angle))


def along(parts, table_real, table_imag, spec):
    def product(data, table):
        return jnp.einsum(
            spec,
            data,
            table,
            precision=lax.Precision.HIGHEST,
            preferred_element_type=jnp.float32,
        )

    return jnp.stack(
        [
            product(parts[0], table_real) - product(parts[1], table_imag),
            product(parts[0], table_imag) + product(parts[1], table_real),
        ]
    )


def dense_shards(
    resident_rows,
    resident_columns,
    resident_strength,
    crossing_rows,
    crossing_columns,
    crossing_strength,
    crossing_count,
):
    cells_x = NX // lax.axis_size("gx")
    cells_y = NY // lax.axis_size("gy")
    slot_count = crossing_rows.shape[-1]
    slot_index = lax.broadcasted_iota(jnp.int32, (1, slot_count), 1)
    live_slot = (slot_index < crossing_count).astype(jnp.float32)
    outgoing = jnp.concatenate(
        [
            crossing_rows.reshape(1, slot_count).astype(jnp.float32),
            crossing_columns.reshape(1, slot_count).astype(jnp.float32),
            crossing_strength.reshape(3, slot_count) * live_slot,
        ],
        axis=0,
    )
    arrived = from_behind(outgoing, "gx", 1)
    resident_ids = resident_rows.reshape(-1) * cells_x + resident_columns.reshape(-1)
    arrived_ids = arrived[0].astype(jnp.int32) * cells_x + arrived[1].astype(jnp.int32)
    cell_ids = jnp.concatenate([resident_ids, arrived_ids])
    weights = jnp.concatenate([resident_strength.reshape(3, -1), arrived[2:]], axis=1)
    cell_total = LEV * cells_y * cells_x
    deposited = jnp.stack(
        [
            jax.ops.segment_sum(weights[component], cell_ids, num_segments=cell_total)
            for component in range(3)
        ]
    )
    vorticity = deposited.reshape(1, 3, LEV, cells_y, cells_x) * (1.0 / math.sqrt(NX * NY))
    parts = vorticity
    for axis, cells, spec in (
        ("gx", cells_x, "clyx,kx->clyk"),
        ("gy", cells_y, "clyx,ky->clkx"),
    ):
        bits = lax.axis_size(axis).bit_length() - 1
        slab_index = lax.axis_index(axis)
        for bit_number in range(bits - 1, -1, -1):
            partner = partner_2(parts, axis, bit_number)
            parts = section_mix(parts, partner, slab_index, bit_number)
        table_real, table_imag = local_table(bit_reverse(slab_index, bits), 1 << bits, cells)
        parts = along(parts, table_real, table_imag, spec)
    return parts


def bin_key(rows, columns, cells_x):
    column = (columns & 1) * (cells_x // 2) + (columns >> 1)
    bin_index = (column // BIN_COLS) * 4 + (rows & 3)
    return bin_index * (BIN_ROWS * BIN_COLS) + (rows >> 2) * BIN_COLS + column % BIN_COLS


def deposit(sources, signs, cells_x, cells_y, residents, base_mesh, after):
    count = len(sources)
    row_bins = cells_y // BIN_ROWS
    column_bins = GROUP
    group_bins = row_bins * column_bins
    width = sources[0].shape[-1]
    first_start = width - LANES
    arrivals = first_start - residents
    window = CHUNK + LANES
    shift = BIN_COLS.bit_length() - 1
    based = base_mesh is not None

    def kernel(signs_ref, *refs):
        source_refs = refs[:count]
        base_ref = refs[count] if based else None
        out_ref, starts_ref, sems = refs[-3:]
        group = pl.program_id(0)

        @pl.when(group == 0)
        def _():
            copies = [
                pltpu.make_async_copy(
                    source_refs[s].at[:, pl.ds(first_start, LANES)],
                    starts_ref.at[s],
                    sems.at[s],
                )
                for s in range(count)
            ]
            for copy in copies:
                copy.start()
            for copy in copies:
                copy.wait()

        scale, unscale = starts_ref[0, 2, 0], starts_ref[0, 3, 0]
        for s in range(1, count):
            scale = jnp.minimum(scale, starts_ref[s, 2, 0])
            unscale = jnp.maximum(unscale, starts_ref[s, 3, 0])
        spans = []
        steps = jnp.int32(0)
        for b in range(group_bins):
            bin_index = group * group_bins + b
            for s in range(count):
                begin, begin_2 = (starts_ref[s, i, bin_index].astype(jnp.int32) for i in (0, 1))
                end, end_2 = (starts_ref[s, i, bin_index + 1].astype(jnp.int32) for i in (0, 1))
                length, length_2 = end - begin, end_2 - begin_2
                spans.append((begin, length, begin_2, length_2))
                steps = jnp.maximum(steps, (length + length_2 + CHUNK - 1) // CHUNK)
                steps = jnp.maximum(steps, (length_2 + LANES - 1) // LANES)
        lane = lax.broadcasted_iota(jnp.int32, (1, CHUNK), 1)
        tail_lane = lax.broadcasted_iota(jnp.int32, (1, LANES), 1)

        def ramp(length):
            return (
                lax.broadcasted_iota(jnp.int32, (length, CHUNK), 0)
                .astype(jnp.float32)
                .astype(jnp.bfloat16)
            )

        row_ramp, col_ramp = ramp(BIN_ROWS), ramp(BIN_COLS)
        one, zero = jnp.bfloat16(1), jnp.bfloat16(0)

        def rolled(source_ref, place, low, high, size, lead):
            offset = low + jnp.minimum((place - low) // LANES * LANES, high - low - size)
            block = source_ref[:, pl.ds(pl.multiple_of(offset, LANES), size)]
            return pltpu.roll(block, lax.rem(2 * size + lead - (place - offset), size), 1)

        def bin_total(step, b):
            base = (group * group_bins + b) * (BIN_ROWS * BIN_COLS)
            hits, weights = [], []
            for s in range(count):
                begin, length, begin_2, length_2 = spans[b * count + s]
                done_2 = jnp.minimum(length_2, step * LANES)
                now_2 = jnp.minimum(length_2 - done_2, LANES)
                done = jnp.minimum(length, step * CHUNK - done_2)
                now = jnp.minimum(length - done, CHUNK - now_2)
                block = rolled(source_refs[s], begin + done, 0, residents, window, 0)[:, :CHUNK]
                tail = rolled(
                    source_refs[s],
                    residents + begin_2 + done_2,
                    residents,
                    residents + arrivals,
                    2 * LANES,
                    LANES - now_2,
                )[:, :LANES]
                tail = jnp.where(tail_lane >= LANES - now_2, tail, block[:, CHUNK - LANES :])
                block = jnp.concatenate([block[:, : CHUNK - LANES], tail], axis=1)
                local = block[0:1].astype(jnp.int32) - base
                row = jnp.where(
                    (lane < now) | (lane >= CHUNK - now_2),
                    lax.shift_right_arithmetic(local, shift),
                    -1,
                )
                col = local & (BIN_COLS - 1)
                row = row.astype(jnp.float32).astype(jnp.bfloat16)
                col = col.astype(jnp.float32).astype(jnp.bfloat16)
                hits.append(jnp.where(row_ramp == row, one, zero).astype(F8))
                mask = col_ramp == col
                pieces, rest = [], block * (signs_ref[s] * scale)
                for _ in range(PIECES):
                    piece = rest.astype(F8).astype(jnp.float32)
                    pieces.append(piece.astype(jnp.bfloat16))
                    rest = (rest - piece) * STEP
                weights.append(
                    jnp.concatenate(
                        [
                            jnp.where(
                                mask,
                                jnp.broadcast_to(piece[k : k + 1], (BIN_COLS, CHUNK)),
                                zero,
                            )
                            for piece in pieces
                            for k in (1, 2, 3)
                        ],
                        axis=0,
                    ).astype(F8)
                )
            total = lax.dot_general(
                jnp.concatenate(weights, axis=1),
                jnp.concatenate(hits, axis=1),
                (((1,), (1,)), ((), ())),
                preferred_element_type=jnp.float32,
            )
            total = total.reshape(PIECES, 3, BIN_COLS, BIN_ROWS)
            result = total[PIECES - 1]
            for piece in range(PIECES - 2, -1, -1):
                result = result * (1.0 / STEP) + total[piece]
            return result * unscale

        def cells_of(b):
            col_bin, row_bin = b // row_bins, b % row_bins
            return (
                slice(None),
                slice(col_bin * BIN_COLS, (col_bin + 1) * BIN_COLS),
                slice(row_bin * BIN_ROWS, (row_bin + 1) * BIN_ROWS),
            )

        def body(step, carry):
            totals = [bin_total(step, b) for b in range(group_bins)]
            for b in range(group_bins):
                out_ref[cells_of(b)] += totals[b]
            return carry

        for b in range(group_bins):
            total = bin_total(0, b)
            out_ref[cells_of(b)] = total + base_ref[cells_of(b)] if based else total
        lax.fori_loop(1, steps, body, 0)

    flops = count * width * BIN_ROWS * BIN_COLS * 24
    out_spec = pl.BlockSpec((3, column_bins * BIN_COLS, cells_y), lambda g: (0, g, 0))
    return pl.pallas_call(
        kernel,
        grid=(cells_x // (column_bins * BIN_COLS),),
        in_specs=[pl.BlockSpec(memory_space=pltpu.SMEM)]
        + [pl.BlockSpec(memory_space=pltpu.VMEM)] * count
        + [out_spec] * based
        + [pl.BlockSpec(memory_space=pl.ANY)] * len(after),
        out_specs=out_spec,
        out_shape=jax.ShapeDtypeStruct((3, cells_x, cells_y), jnp.float32),
        scratch_shapes=[
            pltpu.SMEM((count, 4, LANES), jnp.float32),
            pltpu.SemaphoreType.DMA((count,)),
        ],
        compiler_params=pltpu.CompilerParams(vmem_limit_bytes=12 << 20),
        cost_estimate=pl.CostEstimate(
            flops=flops, bytes_accessed=12 * cells_x * cells_y, transcendentals=0
        ),
        name="deposit",
    )(signs, *sources, *([base_mesh] if based else []), *after)


def turns(numerator, total):
    angle = (numerator % total).astype(jnp.float32) * (TWO_PI / total)
    return jnp.cos(angle), -jnp.sin(angle)


def stage_table(radix, length):
    k = np.arange(length)[None, :, None]
    n = radix * np.arange(length)[None, None, :] + np.arange(radix)[:, None, None]
    angle = (k * n % (radix * length)) * (-TWO_PI / (radix * length))
    real, imag = np.cos(angle), np.sin(angle)
    table = np.concatenate(
        [np.concatenate([real, -imag], axis=2), np.concatenate([imag, real], axis=2)], axis=1
    )
    high = table.astype(ml_dtypes.bfloat16)
    low = (table - high.astype(np.float64)).astype(ml_dtypes.bfloat16)
    return jnp.asarray(np.concatenate([high, low], axis=2))


def tripled(held_ref, residue):
    length = held_ref.shape[1]
    high = held_ref[residue, :, :length]
    return jnp.concatenate([high, high, held_ref[residue, :, length:]], axis=1)


def phases(k_first, radix, length, total):
    place = lax.iota(jnp.int32, radix * length)
    return turns(k_first * (radix * (place % length) + place // length), total)


def split(value):
    high = value.astype(jnp.bfloat16)
    return high, (value - high.astype(jnp.float32)).astype(jnp.bfloat16)


def columns_transform(meshes, scalars, phase, held, component, block):
    count = len(meshes)
    cells_x, cells_y = meshes[0].shape[1:]
    half = cells_x // 2

    def kernel(scalars_ref, phase_ref, held_ref, *refs):
        mesh_refs, out_ref = refs[:count], refs[count]
        lanes = pl.ds(pl.multiple_of(pl.program_id(0) * block, LANES), block)
        pieces = []
        for residue in range(2):
            rows = slice(residue * half, (residue + 1) * half)
            data = [mesh_ref[component, rows, lanes] for mesh_ref in mesh_refs]
            real = sum(scalars_ref[0, i] * data[i] for i in range(count))
            imag = sum(scalars_ref[1, i] * data[i] for i in range(count))
            cosine, sine = (
                jnp.concatenate([phase_ref[i, rows, :]] * (block // LANES), axis=1) for i in (0, 1)
            )
            real, imag = real * cosine - imag * sine, real * sine + imag * cosine
            high, low = split(jnp.concatenate([real, imag], axis=0))
            pieces.append(
                jnp.dot(
                    tripled(held_ref, residue),
                    jnp.concatenate([high, low, high], axis=0),
                    preferred_element_type=jnp.float32,
                )
            )
        for part in range(2):
            rows = slice(part * half, (part + 1) * half)
            out_ref[part, 0, :half] = pieces[0][rows] + pieces[1][rows]
            out_ref[part, 0, half:] = pieces[0][rows] - pieces[1][rows]

    return pl.pallas_call(
        kernel,
        grid=(cells_y // block,),
        in_specs=[
            pl.BlockSpec(memory_space=pltpu.SMEM),
            pl.BlockSpec(memory_space=pltpu.VMEM),
            pl.BlockSpec(memory_space=pltpu.VMEM),
        ]
        + [pl.BlockSpec(memory_space=pltpu.VMEM)] * count,
        out_specs=pl.BlockSpec((2, 1, cells_x, block), lambda g: (0, 0, 0, g)),
        out_shape=jax.ShapeDtypeStruct((2, 1, cells_x, cells_y), jnp.float32),
        compiler_params=pltpu.CompilerParams(vmem_limit_bytes=12 << 20),
        cost_estimate=pl.CostEstimate(
            flops=12 * cells_x * cells_x * cells_y,
            bytes_accessed=(count + 2) * 4 * cells_x * cells_y,
            transcendentals=0,
        ),
        name="columns_transform",
    )(scalars, phase, held, *meshes)


def rows_transform(own, partner, scalars, held, block, component, count, result):
    cells_x, cells_y = own.shape[2:]
    quarter = cells_y // 4

    def kernel(scalars_ref, held_ref, own_ref, partner_ref, *refs):
        out_ref = refs[-1]
        pieces = []
        for residue in range(4):
            where = slice(residue * quarter, (residue + 1) * quarter)
            own_real, own_imag = scalars_ref[0:1, where], scalars_ref[1:2, where]
            other_real, other_imag = scalars_ref[2:3, where], scalars_ref[3:4, where]
            a, b = own_ref[0, 0, :, where], own_ref[1, 0, :, where]
            d, e = partner_ref[0, 0, :, where], partner_ref[1, 0, :, where]
            real = own_real * a - own_imag * b + other_real * d - other_imag * e
            imag = own_real * b + own_imag * a + other_real * e + other_imag * d
            high, low = split(jnp.concatenate([real, imag], axis=1))
            piece = lax.dot_general(
                tripled(held_ref, residue),
                jnp.concatenate([high, low, high], axis=1),
                (((1,), (1,)), ((), ())),
                preferred_element_type=jnp.float32,
            )
            pieces.append((piece[:quarter], piece[quarter:]))
        (ar, ai), (br, bi), (cr, ci), (dr, di) = pieces
        even_r, even_i, odd_r, odd_i = ar + cr, ai + ci, br + dr, bi + di
        diff_r, diff_i, turn_r, turn_i = ar - cr, ai - ci, br - dr, bi - di
        out_ref[0, 0, 0, 0 * quarter : 1 * quarter] = even_r + odd_r
        out_ref[1, 0, 0, 0 * quarter : 1 * quarter] = even_i + odd_i
        out_ref[0, 0, 0, 1 * quarter : 2 * quarter] = diff_r + turn_i
        out_ref[1, 0, 0, 1 * quarter : 2 * quarter] = diff_i - turn_r
        out_ref[0, 0, 0, 2 * quarter : 3 * quarter] = even_r - odd_r
        out_ref[1, 0, 0, 2 * quarter : 3 * quarter] = even_i - odd_i
        out_ref[0, 0, 0, 3 * quarter : 4 * quarter] = diff_r - turn_i
        out_ref[1, 0, 0, 3 * quarter : 4 * quarter] = diff_i + turn_r

    spec = pl.BlockSpec((2, 1, block, cells_y), lambda g: (0, 0, g, 0))
    chained = result is not None
    return pl.pallas_call(
        kernel,
        grid=(cells_x // block,),
        in_specs=[
            pl.BlockSpec(memory_space=pltpu.VMEM),
            pl.BlockSpec(memory_space=pltpu.VMEM),
            spec,
            spec,
        ]
        + [pl.BlockSpec(memory_space=pl.ANY)] * chained,
        out_specs=pl.BlockSpec(
            (2, 1, 1, cells_y, block), lambda g: (0, component, 0, 0, g)
        ),
        out_shape=jax.ShapeDtypeStruct((2, count, 1, cells_y, cells_x), jnp.float32),
        input_output_aliases={4: 0} if chained else {},
        compiler_params=pltpu.CompilerParams(vmem_limit_bytes=24 << 20),
        cost_estimate=pl.CostEstimate(
            flops=6 * cells_y * cells_y * cells_x,
            bytes_accessed=24 * cells_x * cells_y,
            transcendentals=0,
        ),
        name="rows_transform",
    )(scalars, held, own, partner, *([result] if chained else []))


def particle_shards(
    resident_rows,
    resident_columns,
    resident_strength,
    crossing_rows,
    crossing_columns,
    crossing_strength,
    crossing_count,
):
    cells_x = NX // lax.axis_size("gx")
    cells_y = NY // lax.axis_size("gy")
    bins = (cells_y // BIN_ROWS) * (cells_x // BIN_COLS)
    gx, gy = lax.axis_index("gx"), lax.axis_index("gy")
    x, z = gx & 1, gx >> 1
    core, y = gy & 1, gy >> 1
    kx_first = bit_reverse(gx, 3)
    ky_first = bit_reverse(gy, 2)

    bin_cells = BIN_ROWS * BIN_COLS
    slot_count = crossing_rows.shape[-1]
    live_slot = lax.iota(jnp.int32, slot_count) < crossing_count.reshape(1)
    key = bin_key(crossing_rows, crossing_columns, cells_x).reshape(-1)
    key = jnp.where(live_slot, key, bins * bin_cells)
    outgoing = lax.sort(
        (key, *(jnp.where(live_slot, crossing_strength[i].reshape(-1), 0.0) for i in range(3))),
        num_keys=1,
        is_stable=False,
    )
    outgoing = jnp.stack([outgoing[0].astype(jnp.float32), *outgoing[1:]])
    arrived = from_behind(outgoing, "gx", 1)
    key = bin_key(resident_rows, resident_columns, cells_x).reshape(-1)
    residents = key.shape[0]
    key, *strength = lax.sort(
        (key, *(resident_strength[i].reshape(-1) for i in range(3))), num_keys=1, is_stable=False
    )
    bounds = lax.broadcasted_iota(jnp.int32, (bins + 8, 1), 0) * bin_cells
    starts = jnp.sum((key[None, :] < bounds).astype(jnp.float32), axis=1)
    starts_2 = jnp.sum((arrived[0:1] < bounds.astype(jnp.float32)).astype(jnp.float32), axis=1)
    starts, starts_2 = (jnp.pad(values, (0, LANES - bins - 8)) for values in (starts, starts_2))
    largest = jnp.maximum(jnp.abs(strength[0]), jnp.abs(strength[1]))
    largest = jnp.max(jnp.maximum(largest, jnp.abs(strength[2])))
    largest = jnp.maximum(jnp.maximum(largest, jnp.max(jnp.abs(arrived[1:]))), 1e-30)
    particles = jnp.concatenate(
        [
            jnp.stack([key.astype(jnp.float32), *strength]),
            arrived,
            jnp.stack(
                [
                    starts,
                    starts_2,
                    jnp.broadcast_to(TOP / largest, (LANES,)),
                    jnp.broadcast_to(largest / TOP, (LANES,)),
                ]
            ),
        ],
        axis=1,
    )

    held_x, held_y = stage_table(2, cells_x // 2), stage_table(4, cells_y // 4)
    kx_low = kx_first & 3

    def signs(members):
        values = []
        for side, k in members:
            slab_y = y if side is near else 1 - y
            flips = kx_low * ((z ^ (k >> 1)) >> 1) + y * slab_y
            values.append((1 - 2 * (flips & 1)).astype(jnp.float32))
        return jnp.stack(values)

    near, far, meshes = {0: particles}, {}, {}
    last = []

    def add(*members):
        sources = [side[k] for side, k in members]
        kind = members[0][1] & 3
        meshes[kind] = deposit(
            sources, signs(members), cells_x, cells_y, residents, meshes.get(kind), last
        )
        last[:] = [meshes[kind]]
        hold.kind = kind

    def hold(*moved):
        held = lax.optimization_barrier([last[0]] + [side[k] for side, k in moved])
        last[0] = held[0]
        meshes[hold.kind] = held[0]
        for (side, k), value in zip(moved, held[1:]):
            side[k] = value

    far[0] = flip(near[0], "gy", 2)
    near[1] = flip(near[0], "gx", 1)
    near[4] = flip(near[0], "gx", 4)
    near[2] = flip(near[0], "gx", 2)
    add((near, 0))
    hold((near, 1))
    far[1] = flip(near[1], "gy", 2)
    add((far, 0))
    hold((near, 4), (near, 2))
    far[4] = flip(near[4], "gy", 2)
    near[5] = flip(near[4], "gx", 1)
    near[6] = flip(near[4], "gx", 2)
    far[2] = flip(near[2], "gy", 2)
    near[3] = flip(near[1], "gx", 2)
    add((near, 1), (far, 1))
    hold((far, 4), (near, 6))
    far[5] = flip(far[4], "gx", 1)
    far[6] = flip(near[6], "gy", 2)
    add((near, 4), (far, 4))
    hold((near, 6), (near, 3))
    near[7] = flip(near[6], "gx", 1)
    far[3] = flip(near[3], "gy", 2)
    add((near, 5), (far, 5))
    hold((near, 7))
    far[7] = flip(near[7], "gy", 2)
    add((near, 2), (far, 2), (near, 6), (far, 6))
    add((near, 3), (far, 3), (near, 7), (far, 7))
    meshes = [meshes[kind] for kind in range(4)]
    scalars = []
    for kind in range(4):
        slab_x, slab_z = x ^ (kind & 1), (z ^ (kind >> 1)) & 1
        real, imag = turns(kx_first * slab_x + 2 * kx_low * slab_z, 8)
        scalars.append(jnp.stack([real, imag]) * (1.0 / math.sqrt(NX * NY)))
    scalars = jnp.stack(scalars, axis=1)

    phase = jnp.stack(phases(kx_first, 2, cells_x // 2, NX))
    phase = jnp.broadcast_to(phase[:, :, None], (2, cells_x, LANES))
    owns = [columns_transform(meshes, scalars, phase, held_x, i, 512) for i in range(3)]
    partners = [flip(own, "gy", 1) for own in owns]

    turn_real, turn_imag = turns(ky_first, 4)
    cosine, sine = phases(ky_first, 4, cells_y // 4, NY)
    with_turn = [cosine * turn_real - sine * turn_imag, cosine * turn_imag + sine * turn_real]
    own, other = jnp.stack([cosine, sine]), jnp.stack(with_turn)
    scalars = jnp.concatenate(
        [jnp.where(core == 0, own, other), jnp.where(core == 0, other, own)]
    )
    result = None
    for i in range(3):
        result = rows_transform(owns[i], partners[i], scalars, held_y, 256, i, 3, result)
    return result


def solution(mesh):
    few = mesh.shape["gx"] == 8 and mesh.shape["gy"] == 4
    return jax.shard_map(
        particle_shards if few else dense_shards,
        mesh=mesh,
        in_specs=(
            P("gy", "gx", None),
            P("gy", "gx", None),
            P(None, "gy", "gx", None),
            P("gy", "gx", None),
            P("gy", "gx", None),
            P(None, "gy", "gx", None),
            P("gy", "gx"),
        ),
        out_specs=P(None, None, None, "gy", "gx"),
        check_vma=False,
    )
```
